32 devices in a mesh: tm: 4 (over x, core), tile: 8 (over z, y).
Axes of the slice: x: 2, y: 2, z: 4, core: 2. Of those that a mesh axis runs over, the one named last changes fastest.
Arguments:
- basis: float32 [256, 128, 512], P(None, 'tile'), may hold values from -6 to 6
- diffusion: float32 [4, 128, 512], P('tm', 'tile'), may hold values from 0.12 to 0.24
- drift_x: float32 [4, 128, 512], P('tm', 'tile'), may hold values from -1 to 1
- drift_y: float32 [4, 128, 512], P('tm', 'tile'), may hold values from -1 to 1
- land_sea: int32 [128, 512], P('tile'), may hold values from 0 to 1, as said below
- obs_cells: int32 [4, 512], P('tm'), may hold values from 0 to 65535
- obs_values: float32 [4, 512], P('tm'), may hold values from -72 to 72
Outputs:
- group_coeffs: float32 [4, 2, 256], P('tm')
- end_fields: float32 [4, 128, 512], P('tm', 'tile')
The draws below stay inside these ranges and needn't reach their ends.
Inputs may be any that keep to these rules, and one draw needn't show every extreme that they name: `land_sea`: only 0 and 1; both occur. `obs_cells`: cells may repeat within and across groups.
All inputs are finite; a program needn't handle non-finite values.
Results may differ from the reference program's by a relative error of at most 0.0003.
Values sent between devices are 32-bit elements; how exact they have to be, the bound alone decides.
A program may use at most 128 MiB of HBM per device.

```python
import math
import jax
import jax.numpy as jnp
from jax import lax

K = 256
STEPS = 6
NY = 512
NOBS = 512
NX = 128
G = 4


spread_rows = 1.0


spread_columns = 0.5


reach_cells = 6


island_count = 10


def smooth_weights(spread_value):
    raw = [math.exp(-0.5 * ((offset - reach_cells) / spread_value) ** 2) for offset in range(2 * reach_cells + 1)]
    norm_value = math.sqrt(sum((value * value for value in raw)))
    return [value / norm_value for value in raw]


def smooth_along(values, axis, spread_value):
    weights = smooth_weights(spread_value)
    length = values.shape[axis]
    padded = jnp.concatenate([lax.slice_in_dim(values, length - reach_cells, length, axis=axis), values, lax.slice_in_dim(values, 0, reach_cells, axis=axis)], axis=axis)
    summed = jnp.zeros_like(values)
    for position in range(2 * reach_cells + 1):
        summed = summed + weights[position] * lax.slice_in_dim(padded, position, position + length, axis=axis)
    return summed


def draw_basis(key, part):
    noise = jax.random.normal(key, (K, NX, NY), jnp.float32)
    smoothed = smooth_along(smooth_along(noise, 1, spread_rows), 2, spread_columns)
    return jnp.clip(smoothed, -6.0, 6.0).astype(jnp.float32)


def draw_drift_x(key, part):
    magnitude = jax.random.uniform(key, (G, NX, NY), jnp.float32, 0.7, 1.0)
    signs = (2 * jax.random.randint(jax.random.fold_in(key, 3), (G, 1, 1), 0, 2) - 1).astype(jnp.float32)
    return (magnitude * signs).astype(jnp.float32)


def draw_land_sea(key, part):
    keys = jax.random.split(key, 4)
    shape = (island_count, 1, 1)
    top_row = jax.random.randint(keys[0], shape, 0, NX)
    height = jax.random.randint(keys[1], shape, max(1, NX // 16), NX // 4 + 1)
    first_column = jax.random.randint(keys[2], shape, 0, NY)
    breadth = jax.random.randint(keys[3], shape, max(1, NY // 16), NY // 4 + 1)
    row_ids = jnp.arange(NX, dtype=jnp.int32)[None, :, None]
    column_ids = jnp.arange(NY, dtype=jnp.int32)[None, None, :]
    inside = (row_ids >= top_row) & (row_ids < top_row + height) & (column_ids >= first_column) & (column_ids < first_column + breadth)
    return (1 - jnp.any(inside, axis=0).astype(jnp.int32)).astype(jnp.int32)


def place_ends(drawn, own_key, least, largest):
    spot = [jax.random.randint(jax.random.fold_in(own_key, axis), (), 0, length) for axis, length in enumerate(drawn.shape)]
    longest = drawn.shape.index(max(drawn.shape))
    neighbour = spot[:longest] + [(spot[longest] + 1) % drawn.shape[longest]] + spot[longest + 1:]
    return drawn.at[tuple(spot)].set(least).at[tuple(neighbour)].set(largest)


def level_of(own_key, shape, shards, low, largest):
    def one(dim, shards_of):
        draws = jax.random.uniform(jax.random.fold_in(jax.random.fold_in(own_key, 6), dim), (shards_of,), jnp.float32, low / len(shards), largest / len(shards))
        return jnp.repeat(jnp.exp(draws), shape[dim] // shards_of).reshape((-1,) + (1,) * (len(shape) - dim - 1))

    loudness = one(*shards[0])
    for cut in shards[1:]:
        loudness = loudness * one(*cut)
    return loudness


def bell_draw(rng, dims, deviation, reach, shards=(), kind=jnp.bfloat16):
    factor_of = level_of(rng, dims, shards, -0.22, 0.18) if shards else 1.0
    entries = jax.random.normal(rng, dims, jnp.float32) * deviation * factor_of
    return jnp.minimum(jnp.maximum(entries, -reach), reach).astype(kind)


def setup_inputs(seed: int = 0) -> dict:
    splits = jax.random.split(jax.random.key(seed), 8)
    basis = draw_basis(jax.random.fold_in(splits[7], 71), 0)
    diffusion = jnp.clip(0.12 + 0.12 * jax.random.uniform(splits[1], (G, NX, NY), jnp.float32) ** level_of(splits[1], (G, NX, NY), ((0, 4), (1, 8)), -0.2, 0.2), 0.12, 0.24)
    drift_x = draw_drift_x(jax.random.fold_in(splits[7], 71), 0)
    drift_y = jnp.clip(jax.random.uniform(splits[3], (G, NX, NY), jnp.float32, -1.0, 1.0) * level_of(splits[3], (G, NX, NY), ((0, 4), (1, 8)), -0.4, 0.0), -1.0, 1.0)
    land_sea = draw_land_sea(jax.random.fold_in(splits[7], 71), 0)
    obs_cells = place_ends(jax.random.randint(splits[5], (G, NOBS), 0, NX * NY), jax.random.fold_in(splits[5], 1), 0, (NX * NY) - 1).astype(jnp.int32)
    obs_values = bell_draw(splits[6], (G, NOBS), 12.0, 72.0, ((0, 4),), jnp.float32)
    return dict(basis=basis, diffusion=diffusion, drift_x=drift_x, drift_y=drift_y, land_sea=land_sea, obs_cells=obs_cells, obs_values=obs_values)


q_inverse = 10.0
ridge = 0.1

def precise_dot(first, second):
    return jnp.dot(first, second, precision=lax.Precision.HIGHEST)

def group_terms(basis, sea_mask, inputs):
    diffusion, drift_x, drift_y, cells, values = inputs
    center_gain = 1.0 - 4.0 * diffusion
    east_gain = diffusion * (1.0 - drift_x)
    west_gain = diffusion * (1.0 + drift_x)
    north_gain = diffusion * (1.0 - drift_y)
    south_gain = diffusion * (1.0 + drift_y)
    field = basis
    for section in range(STEPS):
        padded_x = jnp.pad(field, ((0, 0), (1, 1), (0, 0)))
        padded_y = jnp.pad(field, ((0, 0), (0, 0), (1, 1)))
        field = sea_mask * (center_gain * field + east_gain * padded_x[:, 2:] + west_gain * padded_x[:, :-2] + north_gain * padded_y[:, :, 2:] + south_gain * padded_y[:, :, :-2])
    flat_basis = basis.reshape(K, NX * NY)
    propagator = precise_dot(flat_basis, field.reshape(K, NX * NY).T) / jnp.float32(NX * NY)
    obs_rows = jnp.take(flat_basis, cells, axis=1)
    obs_info = precise_dot(obs_rows, obs_rows.T) / jnp.float32(NOBS)
    obs_rhs = precise_dot(obs_rows, values) / jnp.float32(NOBS)
    return (propagator, obs_info, obs_rhs)

def reference(basis, diffusion, drift_x, drift_y, land_sea, obs_cells, obs_values):
    sea_mask = land_sea.astype(jnp.float32)
    propagators, infos, rhs_terms = lax.map(lambda inputs: group_terms(basis, sea_mask, inputs), (diffusion, drift_x, drift_y, obs_cells, obs_values))
    order = (G + 1) * K
    system = jnp.zeros((order, order), jnp.float32)
    right = jnp.zeros((order,), jnp.float32)
    identity = jnp.eye(K, dtype=jnp.float32)
    for group in range(G):
        prop = propagators[group]
        upper = q_inverse * precise_dot(prop.T, prop) + ridge * identity
        cross = -q_inverse * prop.T
        lower = (q_inverse + ridge) * identity + infos[group]
        start = group * K
        system = system.at[start:start + K, start:start + K].add(upper)
        system = system.at[start:start + K, start + K:start + 2 * K].add(cross)
        system = system.at[start + K:start + 2 * K, start:start + K].add(cross.T)
        system = system.at[start + K:start + 2 * K, start + K:start + 2 * K].add(lower)
        right = right.at[start + K:start + 2 * K].add(rhs_terms[group])
    states = jnp.linalg.solve(system, right).reshape(G + 1, K)
    group_coeffs = jnp.stack([states[:-1], states[1:]], axis=1)
    end_fields = jnp.tensordot(states[1:], basis, axes=1, precision=lax.Precision.HIGHEST)
    return (group_coeffs, end_fields)
```

```python
import functools

import jax
import jax.numpy as jnp
from jax import lax
from jax.experimental import pallas as pl
from jax.experimental.pallas import tpu as pltpu
from jax.sharding import PartitionSpec as P

STEPS = 6
HALF = STEPS // 2

q_inverse = 10.0
ridge = 0.1

NT = (((1,), (1,)), ((), ()))
NN = (((1,), (0,)), ((), ()))
TN = (((0,), (0,)), ((), ()))


def split(x):
    high = x.astype(jnp.bfloat16)
    return high, (x - high.astype(jnp.float32)).astype(jnp.bfloat16)


def dot16(a, b, dims):
    return lax.dot_general(a, b, dims, preferred_element_type=jnp.float32)


def dot32(a, b, dims=NN):
    return lax.dot_general(
        a, b, dims, precision=lax.Precision.HIGHEST, preferred_element_type=jnp.float32
    )


def obs_kernel(rows, basis_ref, counts_ref, weights_ref, info_ref, rhs_ref):
    info_ref[...] = jnp.zeros_like(info_ref)
    rhs_ref[...] = jnp.zeros_like(rhs_ref)

    def row(r, _):
        x = basis_ref[r]
        y = x * counts_ref[pl.ds(r, 1), :]
        z = x * weights_ref[pl.ds(r, 1), :]
        xh, xl = split(x)
        yh, yl = split(y)
        info_ref[...] += dot16(xh, yh, NT) + dot16(xh, yl, NT) + dot16(xl, yh, NT)
        part = z[:, :128]
        for c in range(128, z.shape[1], 128):
            part += z[:, c : c + 128]
        rhs_ref[...] += part
        return 0

    lax.fori_loop(0, rows, row, 0)


def stencil_kernel(
    rows, block, basis_ref, halo_ref, fg_ref, lg_ref, prop_ref, gf, gl, f1, l1, f2, l2, fh, fl, lh, ll
):
    width, columns = basis_ref.shape[1:]
    halves = block // 8
    for which, (src, dst) in enumerate(((fg_ref, gf), (lg_ref, gl))):
        for i in range(5):
            for r in range(src.shape[1]):
                dst[i, r] = jnp.broadcast_to(src[i, r : r + 1, :], (8, columns))

    def rolled(x):
        return pltpu.roll(x, columns - 1, 1), pltpu.roll(x, 1, 1)

    def update(g, r, center, east, west, north, south):
        return (
            g[0, r] * center + g[1, r] * east + g[2, r] * west + g[3, r] * north + g[4, r] * south
        )

    def fields(kb, _):
        k = pl.multiple_of(kb * block, block)

        def load(r, h):
            if r < 0:
                return halo_ref[r + HALF, pl.ds(k + 8 * h, 8), :]
            if r >= rows:
                return halo_ref[r - rows + HALF, pl.ds(k + 8 * h, 8), :]
            return basis_ref[r, pl.ds(k + 8 * h, 8), :]

        edge = HALF - 1
        before = [load(-edge - 1, h) for h in range(halves)]
        here = [load(-edge, h) for h in range(halves)]
        for r in range(-edge, rows + edge):
            after = [load(r + 1, h) for h in range(halves)]
            for h in range(halves):
                north, south = rolled(here[h])
                f1[r + edge, h] = update(gf, r + edge, here[h], after[h], before[h], north, south)
                l1[r + edge, h] = update(gl, r + edge, here[h], after[h], before[h], north, south)
            before, here = here, after
        for g, s1, s2, high, low in ((gf, f1, f2, fh, fl), (gl, l1, l2, lh, ll)):
            src, dst = s1, s2
            for step in range(1, HALF):
                reach = HALF - 1 - step
                before = [src[edge - reach - 1, h] for h in range(halves)]
                here = [src[edge - reach, h] for h in range(halves)]
                for r in range(-reach, rows + reach):
                    after = [src[r + 1 + edge, h] for h in range(halves)]
                    new = []
                    for h in range(halves):
                        north, south = rolled(here[h])
                        new.append(update(g, r + edge, here[h], after[h], before[h], north, south))
                    if step < HALF - 1:
                        for h in range(halves):
                            dst[r + edge, h] = new[h]
                    else:
                        a, b = split(jnp.concatenate(new, axis=0))
                        high[r, pl.ds(k, block), :] = a
                        low[r, pl.ds(k, block), :] = b
                    before, here = here, after
                src, dst = dst, src
        return 0

    lax.fori_loop(0, width // block, fields, 0)
    prop_ref[...] = jnp.zeros_like(prop_ref)

    def row(r, _):
        prop_ref[...] += (
            dot16(lh[r], fh[r], NT) + dot16(lh[r], fl[r], NT) + dot16(ll[r], fh[r], NT)
        )
        return 0

    lax.fori_loop(0, rows, row, 0)


def eye_of(n):
    i = lax.broadcasted_iota(jnp.int32, (n, n), 0)
    j = lax.broadcasted_iota(jnp.int32, (n, n), 1)
    return (i == j).astype(jnp.float32)


def invert(mats, invs, tmps):
    n = mats[0].shape[0]
    eye = eye_of(n)
    size = 0.0
    for a, x, t in zip(mats, invs, tmps):
        scale = 1.0 / jnp.max(jnp.sum(jnp.abs(a[...]), axis=0, keepdims=True))
        r = eye - scale * a[...]
        t[...] = r
        x[...] = scale * (eye + r)
        size = jnp.maximum(size, jnp.sum(r * r))

    def grow(carry):
        it, _ = carry
        size = 0.0
        for x, t in zip(invs, tmps):
            r = dot32(t[...], t[...])
            t[...] = r
            x[...] += dot32(x[...], r)
            size = jnp.maximum(size, jnp.sum(r * r))
        return it + 1, size

    lax.while_loop(lambda c: (c[1] > 1e-4) & (c[0] < 30), grow, (0, size))

    def correct(carry):
        it, _ = carry
        size = 0.0
        for a, x in zip(mats, invs):
            r = eye - dot32(a[...], x[...])
            x[...] += dot32(x[...], r)
            size = jnp.maximum(size, jnp.sum(r * r))
        return it + 1, size

    lax.while_loop(lambda c: (c[1] > 1e-7) & (c[0] < 5), correct, (0, jnp.float32(1.0)))


def join_kernel(groups, scale_prop, scale_obs, prop_ref, info_ref, rhs_ref, out_ref, s, x, t, w):
    n = prop_ref.shape[1]
    middle = groups // 2
    q = q_inverse
    eye = eye_of(n)

    def prop(g):
        return prop_ref[g] * scale_prop

    def diagonal(i):
        value = ridge * eye
        if i < groups:
            p = prop(i)
            value = value + q * dot32(p, p, TN)
        if i > 0:
            value = value + (q * eye + info_ref[i - 1] * scale_obs)
            if i < groups:
                value = value + ridge * eye
        return value

    def right(i):
        if i == 0:
            return jnp.zeros((8, n), jnp.float32)
        return jnp.broadcast_to(rhs_ref[i - 1 : i, :] * scale_obs, (8, n))

    for i in range(groups + 1):
        s[i] = diagonal(i)
    vec = [right(i) for i in range(groups + 1)]
    for level in range(max(middle, groups - middle)):
        top = level if level < middle else None
        low = groups - level if groups - level > middle else None
        todo = [i for i in (top, low) if i is not None]
        invert([s.at[i] for i in todo], [x.at[i] for i in todo], [t.at[i] for i in todo])
        for i in todo:
            if i == top:
                p = prop(i)
                w[i] = q * dot32(x[i], p, NT)
                s[i + 1] -= q * dot32(p, w[i])
                vec[i + 1] = vec[i + 1] + dot32(vec[i], w[i])
            else:
                p = prop(i - 1)
                w[i] = q * dot32(x[i], p)
                s[i - 1] -= q * dot32(p, w[i], TN)
                vec[i - 1] = vec[i - 1] + dot32(vec[i], w[i])
    invert([s.at[middle]], [x.at[middle]], [t.at[middle]])
    state = {middle: dot32(vec[middle], x[middle])}
    for i in range(middle - 1, -1, -1):
        state[i] = dot32(vec[i], x[i]) + dot32(state[i + 1], w[i], NT)
    for i in range(middle + 1, groups + 1):
        state[i] = dot32(vec[i], x[i]) + dot32(state[i - 1], w[i], NT)
    for i in range(groups + 1):
        out_ref[i : i + 1, :] = state[i][:1]


VMEM = pltpu.VMEM


def shift(cells, width, dim):
    count = lax.axis_size("tile")
    head = lax.slice_in_dim(cells, 0, width, axis=dim)
    tail = lax.slice_in_dim(cells, cells.shape[dim] - width, cells.shape[dim], axis=dim)
    return (
        lax.ppermute(tail, "tile", [(i, i + 1) for i in range(count - 1)]),
        lax.ppermute(head, "tile", [(i + 1, i) for i in range(count - 1)]),
    )


def moved(x, by, dim):
    zero = jnp.zeros_like(lax.slice_in_dim(x, 0, 1, axis=dim))
    if by > 0:
        return jnp.concatenate([lax.slice_in_dim(x, 1, x.shape[dim], axis=dim), zero], axis=dim)
    return jnp.concatenate([zero, lax.slice_in_dim(x, 0, x.shape[dim] - 1, axis=dim)], axis=dim)


def shards(basis, diffusion, drift_x, drift_y, land_sea, obs_cells, obs_values):
    width, rows, columns = basis.shape
    nobs = obs_cells.shape[1]
    groups = lax.axis_size("tm")
    tiles = lax.axis_size("tile")
    group = lax.axis_index("tm")

    share = width // groups
    by_row = basis.transpose(1, 0, 2)
    mine = lax.dynamic_slice_in_dim(by_row, group * share, share, axis=1)
    above, below = shift(mine, HALF, 0)
    halo = lax.all_gather(jnp.concatenate([above, below], axis=0), "tm", axis=1, tiled=True)

    cells = jnp.stack(
        [diffusion[0], drift_x[0], drift_y[0], land_sea.astype(jnp.float32)], axis=0
    )
    before, after = shift(cells, HALF, 1)
    cells = jnp.concatenate([before, cells, after], axis=1)
    d, dx, dy, sea = cells[0], cells[1], cells[2], cells[3]
    column = lax.broadcasted_iota(jnp.int32, d.shape, 1)
    center = sea * (1.0 - 4.0 * d)
    east = sea * (d * (1.0 - dx))
    west = sea * (d * (1.0 + dx))
    north = jnp.where(column == columns - 1, 0.0, sea * (d * (1.0 - dy)))
    south = jnp.where(column == 0, 0.0, sea * (d * (1.0 + dy)))
    forward = jnp.stack([center, east, west, north, south])[:, 1:-1]
    backward = jnp.stack(
        [center, moved(west, 1, 0), moved(east, -1, 0), moved(south, 1, 1), moved(north, -1, 1)]
    )[:, 1:-1]

    offset = lax.axis_index("tile") * (rows * columns)
    local = obs_cells[0] - offset
    inside = (local >= 0) & (local < rows * columns)
    row_of = jnp.where(inside, local // columns, -1)
    col_of = local % columns
    in_row = lax.broadcasted_iota(jnp.int32, (rows, nobs), 0) == row_of[None, :]
    in_col = (lax.broadcasted_iota(jnp.int32, (columns, nobs), 0) == col_of[None, :]).astype(
        jnp.float32
    )
    hits = jnp.concatenate(
        [in_row.astype(jnp.float32), jnp.where(in_row, obs_values[0][None, :], 0.0)], axis=0
    )
    hits = dot32(hits, in_col, NT)

    info, rhs = pl.pallas_call(
        functools.partial(obs_kernel, rows),
        out_shape=(
            jax.ShapeDtypeStruct((width, width), jnp.float32),
            jax.ShapeDtypeStruct((width, 128), jnp.float32),
        ),
        in_specs=[pl.BlockSpec(memory_space=VMEM)] * 3,
        out_specs=[pl.BlockSpec(memory_space=VMEM)] * 2,
        compiler_params=pltpu.CompilerParams(vmem_limit_bytes=32 << 20),
        cost_estimate=pl.CostEstimate(
            flops=6 * width * width * rows * columns,
            bytes_accessed=4 * width * rows * columns,
            transcendentals=0,
        ),
        name="obs_info",
    )(by_row, hits[:rows], hits[rows:])

    block = 16
    edge_rows = rows + 2 * (HALF - 1)
    prop = pl.pallas_call(
        functools.partial(stencil_kernel, rows, block),
        out_shape=jax.ShapeDtypeStruct((width, width), jnp.float32),
        in_specs=[pl.BlockSpec(memory_space=VMEM)] * 4,
        out_specs=pl.BlockSpec(memory_space=VMEM),
        scratch_shapes=[VMEM((5, edge_rows, 8, columns), jnp.float32)] * 2
        + [VMEM((edge_rows, block // 8, 8, columns), jnp.float32)] * 4
        + [VMEM((rows, width, columns), jnp.bfloat16)] * 4,
        compiler_params=pltpu.CompilerParams(vmem_limit_bytes=48 << 20),
        cost_estimate=pl.CostEstimate(
            flops=66 * width * rows * columns,
            bytes_accessed=4 * width * rows * columns,
            transcendentals=0,
        ),
        name="propagate",
    )(by_row, halo, forward, backward)

    packed = jnp.concatenate([prop, info, jnp.sum(rhs, axis=1)[None, :]], axis=0)
    packed = lax.psum(packed, "tile")
    packed = lax.all_gather(packed, "tm", axis=0)
    states = pl.pallas_call(
        functools.partial(
            join_kernel, groups, 1.0 / (rows * columns * tiles), 1.0 / nobs
        ),
        out_shape=jax.ShapeDtypeStruct((groups + 1, width), jnp.float32),
        in_specs=[pl.BlockSpec(memory_space=VMEM)] * 3,
        out_specs=pl.BlockSpec(memory_space=VMEM),
        scratch_shapes=[VMEM((groups + 1, width, width), jnp.float32)] * 4,
        compiler_params=pltpu.CompilerParams(vmem_limit_bytes=48 << 20),
        name="join",
    )(packed[:, :width], packed[:, width : 2 * width], packed[:, 2 * width])
    coeffs = lax.dynamic_slice_in_dim(states, group, 2, axis=0)
    end_fields = jnp.sum(coeffs[1][:, None, None] * basis, axis=0)
    return coeffs[None], end_fields[None]


def solution(mesh):
    in_specs = (
        P(None, "tile", None),
        P("tm", "tile", None),
        P("tm", "tile", None),
        P("tm", "tile", None),
        P("tile", None),
        P("tm", None),
        P("tm", None),
    )
    out_specs = (P("tm", None, None), P("tm", "tile", None))
    return jax.shard_map(shards, mesh=mesh, in_specs=in_specs, out_specs=out_specs, check_vma=False)
```

```python
import functools

import jax
import jax.numpy as jnp
from jax import lax
from jax.experimental import pallas as pl
from jax.experimental.pallas import tpu as pltpu
from jax.sharding import PartitionSpec as P

STEPS = 6
HALF = STEPS // 2

q_inverse = 10.0
ridge = 0.1

NT = (((1,), (1,)), ((), ()))
NN = (((1,), (0,)), ((), ()))
TN = (((0,), (0,)), ((), ()))


def split(x):
    high = x.astype(jnp.bfloat16)
    return high, (x - high.astype(jnp.float32)).astype(jnp.bfloat16)


def dot16(a, b, dims):
    return lax.dot_general(a, b, dims, preferred_element_type=jnp.float32)


def dot32(a, b, dims=NN):
    return lax.dot_general(
        a, b, dims, precision=lax.Precision.HIGHEST, preferred_element_type=jnp.float32
    )


def dot3(a, b):
    ah, al = split(a)
    bh, bl = split(b)
    return dot16(ah, bh, NN) + dot16(ah, bl, NN) + dot16(al, bh, NN)


MESH = pl.DeviceIdType.MESH


def remote(src, dst, send, recv, **where):
    return pltpu.make_async_remote_copy(
        src_ref=src, dst_ref=dst, send_sem=send, recv_sem=recv, device_id=where, device_id_type=MESH
    )


def edge_kernel(
    chips, tiles, basis_ref, cells_ref, counts_ref, weights_ref, halo_ref, fringe_ref, info_ref,
    rhs_ref, edge, xh, xl, first_send, first_recv, cell_send, cell_recv, over_send, over_recv,
    mate_send, mate_recv,
):
    width, rows, columns = basis_ref.shape
    group, tile = lax.axis_index("tm"), lax.axis_index("tile")
    chip, core = group // 2, group % 2
    mate = group + 1 - 2 * core
    share = edge.shape[1]
    mine = pl.multiple_of(group * share, share)
    others = [((chip + i) % chips) * 2 + core for i in range(1, chips)]
    has = (tile > 0, tile < tiles - 1)
    near = (tile - 1, tile + 1)

    barrier = pltpu.get_barrier_semaphore()
    for peer in others + [mate]:
        pl.semaphore_signal(barrier, inc=1, device_id={"tm": peer}, device_id_type=MESH)
    for peer in ((tile + tiles - 1) % tiles, (tile + 1) % tiles):
        pl.semaphore_signal(barrier, inc=1, device_id={"tile": peer}, device_id_type=MESH)

    def cut(j, _):
        x = basis_ref[pl.ds(mine + 8 * j, 8)]
        y = jnp.swapaxes(x, 0, 1)
        k = pl.multiple_of(8 * j, 8)
        edge[:HALF, pl.ds(k, 8), :] = y[:HALF]
        edge[HALF:, pl.ds(k, 8), :] = y[rows - HALF :]
        return 0

    lax.fori_loop(0, share // 8, cut, 0)
    pl.semaphore_wait(barrier, chips + 2)

    def part(side, k):
        return halo_ref.at[pl.ds(side * HALF, HALF), pl.ds(pl.multiple_of(k, share), share), :]

    def send(side):
        other = 1 - side
        first = 0 if side == 0 else rows - HALF
        return (
            remote(edge.at[pl.ds(side * HALF, HALF)], part(other, mine), first_send.at[side],
                   first_recv.at[other], tile=near[side]),
            remote(cells_ref.at[pl.ds(first, HALF)], fringe_ref.at[pl.ds(other * HALF, HALF)],
                   cell_send.at[side], cell_recv.at[other], tile=near[side]),
        )

    def arrival(side):
        return (
            remote(edge.at[pl.ds(side * HALF, HALF)], part(side, mine), first_send.at[side],
                   first_recv.at[side], tile=near[side]),
            remote(cells_ref.at[pl.ds(0, HALF)], fringe_ref.at[pl.ds(side * HALF, HALF)],
                   cell_send.at[side], cell_recv.at[side], tile=near[side]),
        )

    def over(side, i):
        return remote(part(side, mine), part(side, mine), over_send.at[side, i],
                      over_recv.at[side, i], tm=others[i])

    def to_mate(side, i):
        k = (((chip - i + chips) % chips) * 2 + core) * share
        return remote(part(side, k), part(side, k), mate_send.at[side, i], mate_recv.at[side, i],
                      tm=mate)

    for side in range(2):

        @pl.when(has[side])
        def _():
            for copy in send(side):
                copy.start()

        @pl.when(jnp.logical_not(has[side]))
        def _():
            halo_ref[side * HALF : (side + 1) * HALF] = jnp.zeros(
                (HALF, width, columns), jnp.float32
            )
            fringe_ref[side * HALF : (side + 1) * HALF] = jnp.zeros(
                (HALF,) + fringe_ref.shape[1:], jnp.float32
            )

    def turn(j, _):
        k = pl.multiple_of(16 * j, 16)
        y = jnp.swapaxes(basis_ref[pl.ds(k, 16)], 0, 1)
        high, low = split(y)
        xh[:, pl.ds(k, 16), :] = high
        xl[:, pl.ds(k, 16), :] = low
        return 0

    lax.fori_loop(0, width // 16, turn, 0)
    info_ref[...] = jnp.zeros_like(info_ref)
    rhs_ref[...] = jnp.zeros_like(rhs_ref)

    def row(r, _):
        a, b = xh[r], xl[r]
        x = a.astype(jnp.float32) + b.astype(jnp.float32)
        yh, yl = split(x * counts_ref[pl.ds(r, 1), :])
        z = x * weights_ref[pl.ds(r, 1), :]
        info_ref[...] += dot16(a, yh, NT) + dot16(a, yl, NT) + dot16(b, yh, NT)
        part_sum = z[:, :128]
        for c in range(128, columns, 128):
            part_sum += z[:, c : c + 128]
        rhs_ref[...] += part_sum
        return 0

    lax.fori_loop(0, rows // 2, row, 0)
    for side in range(2):

        @pl.when(has[side])
        def _():
            arrival(side)[0].wait_recv()
            for i in range(chips - 1):
                over(side, i).start()
            to_mate(side, 0).start()

    lax.fori_loop(rows // 2, rows, row, 0)
    for side in range(2):

        @pl.when(has[side])
        def _():
            for i in range(chips - 1):
                over(side, i).wait_recv()
                to_mate(side, i + 1).start()

    for side in range(2):

        @pl.when(has[side])
        def _():
            for i in range(chips):
                to_mate(side, i).wait_recv()
                to_mate(side, i).wait_send()
            for i in range(chips - 1):
                over(side, i).wait_send()
            arrival(side)[1].wait_recv()
            for copy in send(side):
                copy.wait_send()


def spread_kernel(chips, tiles, part_ref, out_ref, land, s1, r1, s2, r2, s3, r3, s4, r4):
    rows = part_ref.shape[0] // tiles
    group, tile = lax.axis_index("tm"), lax.axis_index("tile")
    chip, core = group // 2, group % 2
    mate = group + 1 - 2 * core
    others = [((chip + i) % chips) * 2 + core for i in range(1, chips)]
    far = [(tile + d) % tiles for d in range(1, tiles)]

    barrier = pltpu.get_barrier_semaphore()
    for peer in others + [mate]:
        pl.semaphore_signal(barrier, inc=1, device_id={"tm": peer}, device_id_type=MESH)
    for peer in far:
        pl.semaphore_signal(barrier, inc=1, device_id={"tile": peer}, device_id_type=MESH)
    pl.semaphore_wait(barrier, chips + tiles - 1)

    def lines(t):
        return pl.ds(pl.multiple_of(t * rows, rows), rows)

    def slot(g, t):
        return out_ref.at[g, lines(t), :]

    def scatter(d):
        return remote(part_ref.at[lines(far[d]), :], land.at[d], s1.at[d], r1.at[d], tile=far[d])

    def gather(d):
        return remote(slot(group, tile), slot(group, tile), s2.at[d], r2.at[d], tile=far[d])

    def held(d):
        return (tile - d + tiles) % tiles

    def over(d, i):
        place = slot(group, held(d))
        return remote(place, place, s3.at[d, i], r3.at[d, i], tm=others[i])

    def to_mate(d, i):
        place = slot(((chip - i + chips) % chips) * 2 + core, held(d))
        return remote(place, place, s4.at[d, i], r4.at[d, i], tm=mate)

    for d in range(tiles - 1):
        scatter(d).start()
    total = part_ref[lines(tile), :]
    for d in range(tiles - 1):
        scatter(d).wait_recv()
        total = total + land[d]
    out_ref[group, lines(tile), :] = total
    for d in range(tiles - 1):
        gather(d).start()
    for d in range(tiles):
        if d:
            gather(d - 1).wait_recv()
        for i in range(chips - 1):
            over(d, i).start()
        to_mate(d, 0).start()
    for d in range(tiles):
        for i in range(chips - 1):
            over(d, i).wait_recv()
            to_mate(d, i + 1).start()
    for d in range(tiles):
        for i in range(chips):
            to_mate(d, i).wait_recv()
            to_mate(d, i).wait_send()
        for i in range(chips - 1):
            over(d, i).wait_send()
    for d in range(tiles - 1):
        scatter(d).wait_send()
        gather(d).wait_send()


def stencil_kernel(
    rows, block, basis_ref, halo_ref, fg_ref, lg_ref, prop_ref, turned, gf, gl, f1, l1, f2, l2, fh, fl, lh, ll
):
    width, _, columns = basis_ref.shape
    halves = block // 8
    for which, (src, dst) in enumerate(((fg_ref, gf), (lg_ref, gl))):
        for i in range(5):
            for r in range(src.shape[1]):
                dst[i, r] = jnp.broadcast_to(src[i, r : r + 1, :], (8, columns))

    def rolled(x):
        return pltpu.roll(x, columns - 1, 1), pltpu.roll(x, 1, 1)

    def update(g, r, center, east, west, north, south):
        return (
            g[0, r] * center + g[1, r] * east + g[2, r] * west + g[3, r] * north + g[4, r] * south
        )

    def fields(kb, _):
        k = pl.multiple_of(kb * block, block)

        def load(r, h):
            if r < 0:
                return halo_ref[r + HALF, pl.ds(k + 8 * h, 8), :]
            if r >= rows:
                return halo_ref[r - rows + HALF, pl.ds(k + 8 * h, 8), :]
            return turned[r, h]

        for h in range(halves):
            turned[:, h] = jnp.swapaxes(basis_ref[pl.ds(k + 8 * h, 8)], 0, 1)
        edge = HALF - 1
        before = [load(-edge - 1, h) for h in range(halves)]
        here = [load(-edge, h) for h in range(halves)]
        for r in range(-edge, rows + edge):
            after = [load(r + 1, h) for h in range(halves)]
            for h in range(halves):
                north, south = rolled(here[h])
                f1[r + edge, h] = update(gf, r + edge, here[h], after[h], before[h], north, south)
                l1[r + edge, h] = update(gl, r + edge, here[h], after[h], before[h], north, south)
            before, here = here, after
        for g, s1, s2, high, low in ((gf, f1, f2, fh, fl), (gl, l1, l2, lh, ll)):
            src, dst = s1, s2
            for step in range(1, HALF):
                reach = HALF - 1 - step
                before = [src[edge - reach - 1, h] for h in range(halves)]
                here = [src[edge - reach, h] for h in range(halves)]
                for r in range(-reach, rows + reach):
                    after = [src[r + 1 + edge, h] for h in range(halves)]
                    new = []
                    for h in range(halves):
                        north, south = rolled(here[h])
                        new.append(update(g, r + edge, here[h], after[h], before[h], north, south))
                    if step < HALF - 1:
                        for h in range(halves):
                            dst[r + edge, h] = new[h]
                    else:
                        a, b = split(jnp.concatenate(new, axis=0))
                        high[r, pl.ds(k, block), :] = a
                        low[r, pl.ds(k, block), :] = b
                    before, here = here, after
                src, dst = dst, src
        return 0

    lax.fori_loop(0, width // block, fields, 0)
    prop_ref[...] = jnp.zeros_like(prop_ref)

    def row(r, _):
        prop_ref[...] += (
            dot16(lh[r], fh[r], NT) + dot16(lh[r], fl[r], NT) + dot16(ll[r], fh[r], NT)
        )
        return 0

    lax.fori_loop(0, rows, row, 0)


def eye_of(n):
    i = lax.broadcasted_iota(jnp.int32, (n, n), 0)
    j = lax.broadcasted_iota(jnp.int32, (n, n), 1)
    return (i == j).astype(jnp.float32)


def invert(mats, invs, tmps):
    n = mats[0].shape[0]
    eye = eye_of(n)
    size = 0.0
    for a, x, t in zip(mats, invs, tmps):
        scale = 1.0 / jnp.max(jnp.sum(jnp.abs(a[...]), axis=0, keepdims=True))
        r = eye - scale * a[...]
        t[...] = r
        x[...] = scale * (eye + r)
        size = jnp.maximum(size, jnp.sum(r * r))

    def small(c):
        return jnp.logical_not(c[1] <= 1e-4) & (c[0] < 30)

    def grow(carry):
        it, _ = carry
        size = 0.0
        for x, t in zip(invs, tmps):
            r = t[...].astype(jnp.bfloat16)
            r = dot16(r, r, NN)
            t[...] = r
            x[...] += dot16(x[...].astype(jnp.bfloat16), r.astype(jnp.bfloat16), NN)
            size = jnp.maximum(size, jnp.sum(r * r))
        return it + 1, size

    lax.while_loop(small, grow, (0, size))

    def residual():
        size = 0.0
        for a, x, t in zip(mats, invs, tmps):
            r = eye - dot32(a[...], x[...])
            t[...] = r
            size = jnp.maximum(size, jnp.sum(r * r))
        return size

    def grow_exact(carry):
        it, _ = carry
        size = 0.0
        for x, t in zip(invs, tmps):
            r = dot32(t[...], t[...])
            t[...] = r
            x[...] += dot32(x[...], r)
            size = jnp.maximum(size, jnp.sum(r * r))
        return it + 1, size

    def again(_):
        size = 0.0
        for a, x, t in zip(mats, invs, tmps):
            scale = 1.0 / jnp.max(jnp.sum(jnp.abs(a[...]), axis=0, keepdims=True))
            r = eye - scale * a[...]
            t[...] = r
            x[...] = scale * (eye + r)
            size = jnp.maximum(size, jnp.sum(r * r))
        lax.while_loop(small, grow_exact, (0, size))
        return residual()

    size = residual()
    size = lax.cond(size <= 0.25, lambda v: v, again, size)

    def correct(carry):
        it, _ = carry
        for x, t in zip(invs, tmps):
            x[...] += dot3(x[...], t[...])
        return it + 1, residual()

    lax.while_loop(lambda c: (c[1] > 1e-6) & (c[0] < 6), correct, (0, size))
    for x, t in zip(invs, tmps):
        x[...] += dot3(x[...], t[...])


def join_kernel(groups, scale_prop, scale_obs, prop_ref, info_ref, rhs_ref, out_ref, s, x, t, w):
    n = prop_ref.shape[1]
    middle = groups // 2
    q = q_inverse
    eye = eye_of(n)

    def prop(g):
        return prop_ref[g] * scale_prop

    def diagonal(i):
        value = ridge * eye
        if i < groups:
            p = prop(i)
            value = value + q * dot32(p, p, TN)
        if i > 0:
            value = value + (q * eye + info_ref[i - 1] * scale_obs)
            if i < groups:
                value = value + ridge * eye
        return value

    def right(i):
        if i == 0:
            return jnp.zeros((8, n), jnp.float32)
        return jnp.broadcast_to(rhs_ref[i - 1 : i, :] * scale_obs, (8, n))

    for i in range(groups + 1):
        s[i] = diagonal(i)
    vec = [right(i) for i in range(groups + 1)]
    for level in range(max(middle, groups - middle)):
        top = level if level < middle else None
        low = groups - level if groups - level > middle else None
        todo = [i for i in (top, low) if i is not None]
        invert([s.at[i] for i in todo], [x.at[i] for i in todo], [t.at[i] for i in todo])
        for i in todo:
            if i == top:
                p = prop(i)
                w[i] = q * dot32(x[i], p, NT)
                s[i + 1] -= q * dot32(p, w[i])
                vec[i + 1] = vec[i + 1] + dot32(vec[i], w[i])
            else:
                p = prop(i - 1)
                w[i] = q * dot32(x[i], p)
                s[i - 1] -= q * dot32(p, w[i], TN)
                vec[i - 1] = vec[i - 1] + dot32(vec[i], w[i])
    invert([s.at[middle]], [x.at[middle]], [t.at[middle]])
    state = {middle: dot32(vec[middle], x[middle])}
    for i in range(middle - 1, -1, -1):
        state[i] = dot32(vec[i], x[i]) + dot32(state[i + 1], w[i], NT)
    for i in range(middle + 1, groups + 1):
        state[i] = dot32(vec[i], x[i]) + dot32(state[i - 1], w[i], NT)
    for i in range(groups + 1):
        out_ref[i : i + 1, :] = state[i][:1]


VMEM = pltpu.VMEM


def moved(x, by, dim):
    zero = jnp.zeros_like(lax.slice_in_dim(x, 0, 1, axis=dim))
    if by > 0:
        return jnp.concatenate([lax.slice_in_dim(x, 1, x.shape[dim], axis=dim), zero], axis=dim)
    return jnp.concatenate([zero, lax.slice_in_dim(x, 0, x.shape[dim] - 1, axis=dim)], axis=dim)


def shards(basis, diffusion, drift_x, drift_y, land_sea, obs_cells, obs_values):
    width, rows, columns = basis.shape
    nobs = obs_cells.shape[1]
    groups = lax.axis_size("tm")
    tiles = lax.axis_size("tile")
    group = lax.axis_index("tm")

    chips = groups // 2
    zeros = jnp.zeros_like(diffusion[0])
    cells = jnp.stack(
        [diffusion[0], drift_x[0], drift_y[0], land_sea.astype(jnp.float32)] + [zeros] * 4, axis=1
    )
    offset = lax.axis_index("tile") * (rows * columns)
    local = obs_cells[0] - offset
    inside = (local >= 0) & (local < rows * columns)
    row_of = jnp.where(inside, local // columns, -1)
    col_of = local % columns
    in_row = lax.broadcasted_iota(jnp.int32, (rows, nobs), 0) == row_of[None, :]
    in_col = (lax.broadcasted_iota(jnp.int32, (columns, nobs), 0) == col_of[None, :]).astype(
        jnp.float32
    )
    hits = jnp.concatenate(
        [in_row.astype(jnp.float32), jnp.where(in_row, obs_values[0][None, :], 0.0)], axis=0
    )
    hits = dot32(hits, in_col, NT)

    share = width // groups
    DMA = pltpu.SemaphoreType.DMA
    whole = pl.BlockSpec(memory_space=VMEM)
    halo, fringe, info, rhs = pl.pallas_call(
        functools.partial(edge_kernel, chips, tiles),
        out_shape=(
            jax.ShapeDtypeStruct((2 * HALF, width, columns), jnp.float32),
            jax.ShapeDtypeStruct((2 * HALF, 8, columns), jnp.float32),
            jax.ShapeDtypeStruct((width, width), jnp.float32),
            jax.ShapeDtypeStruct((width, 128), jnp.float32),
        ),
        in_specs=[whole] * 4,
        out_specs=[whole] * 4,
        scratch_shapes=[VMEM((2 * HALF, share, columns), jnp.float32)]
        + [VMEM((rows, width, columns), jnp.bfloat16)] * 2
        + [DMA((2,))] * 4
        + [DMA((2, max(chips - 1, 1)))] * 2
        + [DMA((2, chips))] * 2,
        compiler_params=pltpu.CompilerParams(
            vmem_limit_bytes=40 << 20, collective_id=0, has_side_effects=True
        ),
        name="edges",
    )(basis, cells, hits[:rows], hits[rows:])
    info = jnp.concatenate([info, jnp.broadcast_to(jnp.sum(rhs, axis=1)[None, :], (8, width))])
    info = lax.all_gather(lax.psum(info, "tile"), "tm", axis=0)

    cells = jnp.concatenate([fringe[:HALF], cells, fringe[HALF:]], axis=0)
    d, dx, dy, sea = cells[:, 0], cells[:, 1], cells[:, 2], cells[:, 3]
    column = lax.broadcasted_iota(jnp.int32, d.shape, 1)
    center = sea * (1.0 - 4.0 * d)
    east = sea * (d * (1.0 - dx))
    west = sea * (d * (1.0 + dx))
    north = jnp.where(column == columns - 1, 0.0, sea * (d * (1.0 - dy)))
    south = jnp.where(column == 0, 0.0, sea * (d * (1.0 + dy)))
    forward = jnp.stack([center, east, west, north, south])[:, 1:-1]
    backward = jnp.stack(
        [center, moved(west, 1, 0), moved(east, -1, 0), moved(south, 1, 1), moved(north, -1, 1)]
    )[:, 1:-1]

    block = 16
    edge_rows = rows + 2 * (HALF - 1)
    prop = pl.pallas_call(
        functools.partial(stencil_kernel, rows, block),
        out_shape=jax.ShapeDtypeStruct((width, width), jnp.float32),
        in_specs=[pl.BlockSpec(memory_space=VMEM)] * 4,
        out_specs=pl.BlockSpec(memory_space=VMEM),
        scratch_shapes=[VMEM((rows, block // 8, 8, columns), jnp.float32)]
        + [VMEM((5, edge_rows, 8, columns), jnp.float32)] * 2
        + [VMEM((edge_rows, block // 8, 8, columns), jnp.float32)] * 4
        + [VMEM((rows, width, columns), jnp.bfloat16)] * 4,
        compiler_params=pltpu.CompilerParams(vmem_limit_bytes=48 << 20),
        cost_estimate=pl.CostEstimate(
            flops=20000 * width * rows * columns,
            bytes_accessed=4 * width * rows * columns,
            transcendentals=0,
        ),
        name="propagate",
    )(basis, halo, forward, backward)

    props = pl.pallas_call(
        functools.partial(spread_kernel, chips, tiles),
        out_shape=jax.ShapeDtypeStruct((groups, width, width), jnp.float32),
        in_specs=[whole],
        out_specs=whole,
        scratch_shapes=[VMEM((tiles - 1, width // tiles, width), jnp.float32)]
        + [DMA((tiles - 1,))] * 4
        + [DMA((tiles, max(chips - 1, 1)))] * 2
        + [DMA((tiles, chips))] * 2,
        compiler_params=pltpu.CompilerParams(
            vmem_limit_bytes=16 << 20, collective_id=1, has_side_effects=True
        ),
        name="spread",
    )(prop)
    states = pl.pallas_call(
        functools.partial(
            join_kernel, groups, 1.0 / (rows * columns * tiles), 1.0 / nobs
        ),
        out_shape=jax.ShapeDtypeStruct((groups + 1, width), jnp.float32),
        in_specs=[pl.BlockSpec(memory_space=VMEM)] * 3,
        out_specs=pl.BlockSpec(memory_space=VMEM),
        scratch_shapes=[VMEM((groups + 1, width, width), jnp.float32)] * 4,
        compiler_params=pltpu.CompilerParams(vmem_limit_bytes=48 << 20),
        name="join",
    )(props, info[:, :width], info[:, width])
    coeffs = lax.dynamic_slice_in_dim(states, group, 2, axis=0)
    end_fields = jnp.sum(coeffs[1][:, None, None] * basis, axis=0)
    return coeffs[None], end_fields[None]


def solution(mesh):
    in_specs = (
        P(None, "tile", None),
        P("tm", "tile", None),
        P("tm", "tile", None),
        P("tm", "tile", None),
        P("tile", None),
        P("tm", None),
        P("tm", None),
    )
    out_specs = (P("tm", None, None), P("tm", "tile", None))
    return jax.shard_map(shards, mesh=mesh, in_specs=in_specs, out_specs=out_specs, check_vma=False)
```

```python
import functools

import jax
import jax.numpy as jnp
from jax import lax
from jax.experimental import pallas as pl
from jax.experimental.pallas import tpu as pltpu
from jax.sharding import PartitionSpec as P

STEPS = 6
HALF = STEPS // 2

q_inverse = 10.0
ridge = 0.1

NT = (((1,), (1,)), ((), ()))
NN = (((1,), (0,)), ((), ()))
TN = (((0,), (0,)), ((), ()))


def split(x):
    high = x.astype(jnp.bfloat16)
    return high, (x - high.astype(jnp.float32)).astype(jnp.bfloat16)


def dot16(a, b, dims):
    return lax.dot_general(a, b, dims, preferred_element_type=jnp.float32)


def dot32(a, b, dims=NN):
    return lax.dot_general(
        a, b, dims, precision=lax.Precision.HIGHEST, preferred_element_type=jnp.float32
    )


def dot3(a, b, dims=NN):
    ah, al = split(a)
    bh, bl = split(b)
    return dot16(ah, bh, dims) + dot16(ah, bl, dims) + dot16(al, bh, dims)


MESH = pl.DeviceIdType.MESH


def remote(src, dst, send, recv, **where):
    return pltpu.make_async_remote_copy(
        src_ref=src, dst_ref=dst, send_sem=send, recv_sem=recv, device_id=where, device_id_type=MESH
    )


def edge_kernel(
    chips, tiles, basis_ref, d_ref, dx_ref, dy_ref, sea_ref, counts_ref, weights_ref, halo_ref, fringe_ref, info_ref,
    edge, cells_ref, rhs_ref, xh, xl, first_send, first_recv, cell_send, cell_recv, over_send, over_recv,
    mate_send, mate_recv,
):
    width, rows, columns = basis_ref.shape
    group, tile = lax.axis_index("tm"), lax.axis_index("tile")
    chip, core = group // 2, group % 2
    mate = group + 1 - 2 * core
    share = edge.shape[1]
    mine = pl.multiple_of(group * share, share)
    others = [((chip + i) % chips) * 2 + core for i in range(1, chips)]
    has = (tile > 0, tile < tiles - 1)
    near = (tile - 1, tile + 1)

    barrier = pltpu.get_barrier_semaphore()
    for peer in others + [mate]:
        pl.semaphore_signal(barrier, inc=1, device_id={"tm": peer}, device_id_type=MESH)
    for peer in ((tile + tiles - 1) % tiles, (tile + 1) % tiles):
        pl.semaphore_signal(barrier, inc=1, device_id={"tile": peer}, device_id_type=MESH)

    cells_ref[...] = jnp.zeros_like(cells_ref)
    for i, ref in enumerate((d_ref, dx_ref, dy_ref, sea_ref)):
        for r in range(HALF):
            cells_ref[r, i : i + 1, :] = ref[r : r + 1, :]
            last = rows - HALF + r
            cells_ref[HALF + r, i : i + 1, :] = ref[last : last + 1, :]

    def cut(j, _):
        x = basis_ref[pl.ds(mine + 8 * j, 8)]
        y = jnp.swapaxes(x, 0, 1)
        k = pl.multiple_of(8 * j, 8)
        edge[:HALF, pl.ds(k, 8), :] = y[:HALF]
        edge[HALF:, pl.ds(k, 8), :] = y[rows - HALF :]
        return 0

    lax.fori_loop(0, share // 8, cut, 0)
    pl.semaphore_wait(barrier, chips + 2)

    def part(side, k):
        return halo_ref.at[pl.ds(side * HALF, HALF), pl.ds(pl.multiple_of(k, share), share), :]

    def send(side):
        other = 1 - side
        first = side * HALF
        return (
            remote(edge.at[pl.ds(side * HALF, HALF)], part(other, mine), first_send.at[side],
                   first_recv.at[other], tile=near[side]),
            remote(cells_ref.at[pl.ds(first, HALF)], fringe_ref.at[pl.ds(other * HALF, HALF)],
                   cell_send.at[side], cell_recv.at[other], tile=near[side]),
        )

    def arrival(side):
        return (
            remote(edge.at[pl.ds(side * HALF, HALF)], part(side, mine), first_send.at[side],
                   first_recv.at[side], tile=near[side]),
            remote(cells_ref.at[pl.ds(0, HALF)], fringe_ref.at[pl.ds(side * HALF, HALF)],
                   cell_send.at[side], cell_recv.at[side], tile=near[side]),
        )

    def over(side, i):
        return remote(part(side, mine), part(side, mine), over_send.at[side, i],
                      over_recv.at[side, i], tm=others[i])

    def to_mate(side, i):
        k = (((chip - i + chips) % chips) * 2 + core) * share
        return remote(part(side, k), part(side, k), mate_send.at[side, i], mate_recv.at[side, i],
                      tm=mate)

    for side in range(2):

        @pl.when(has[side])
        def _():
            for copy in send(side):
                copy.start()

        @pl.when(jnp.logical_not(has[side]))
        def _():
            halo_ref[side * HALF : (side + 1) * HALF] = jnp.zeros(
                (HALF, width, columns), jnp.float32
            )
            fringe_ref[side * HALF : (side + 1) * HALF] = jnp.zeros(
                (HALF,) + fringe_ref.shape[1:], jnp.float32
            )

    def turn(j, _):
        k = pl.multiple_of(16 * j, 16)
        y = jnp.swapaxes(basis_ref[pl.ds(k, 16)], 0, 1)
        high, low = split(y)
        xh[:, pl.ds(k, 16), :] = high
        xl[:, pl.ds(k, 16), :] = low
        return 0

    lax.fori_loop(0, width // 16, turn, 0)
    info_ref[...] = jnp.zeros_like(info_ref)
    rhs_ref[...] = jnp.zeros_like(rhs_ref)

    def row(r, _):
        a, b = xh[r], xl[r]
        x = a.astype(jnp.float32) + b.astype(jnp.float32)
        yh, yl = split(x * counts_ref[pl.ds(r, 1), :])
        z = x * weights_ref[pl.ds(r, 1), :]
        info_ref[:width, :] += dot16(a, yh, NT) + dot16(a, yl, NT) + dot16(b, yh, NT)
        part_sum = z[:, :128]
        for c in range(128, columns, 128):
            part_sum += z[:, c : c + 128]
        rhs_ref[...] += part_sum
        return 0

    lax.fori_loop(0, rows // 2, row, 0)
    for side in range(2):

        @pl.when(has[side])
        def _():
            arrival(side)[0].wait_recv()
            for i in range(chips - 1):
                over(side, i).start()
            to_mate(side, 0).start()

    lax.fori_loop(rows // 2, rows, row, 0)
    for side in range(2):

        @pl.when(has[side])
        def _():
            for i in range(chips - 1):
                over(side, i).wait_recv()
                to_mate(side, i + 1).start()

    for side in range(2):

        @pl.when(has[side])
        def _():
            for i in range(chips):
                to_mate(side, i).wait_recv()
                to_mate(side, i).wait_send()
            for i in range(chips - 1):
                over(side, i).wait_send()
            arrival(side)[1].wait_recv()
            for copy in send(side):
                copy.wait_send()

    info_ref[width:, :] = dot32(jnp.ones((8, 128), jnp.float32), rhs_ref[...], NT)


def spread_kernel(chips, tiles, part_ref, out_ref, land, s1, r1, s2, r2, s3, r3, s4, r4):
    group, tile = lax.axis_index("tm"), lax.axis_index("tile")
    chip, core = group // 2, group % 2
    mate = group + 1 - 2 * core
    others = [((chip + i) % chips) * 2 + core for i in range(1, chips)]
    far = [(tile + d) % tiles for d in range(1, tiles)]

    barrier = pltpu.get_barrier_semaphore()
    for peer in others + [mate]:
        pl.semaphore_signal(barrier, inc=1, device_id={"tm": peer}, device_id_type=MESH)
    for peer in far:
        pl.semaphore_signal(barrier, inc=1, device_id={"tile": peer}, device_id_type=MESH)
    pl.semaphore_wait(barrier, chips + tiles - 1)

    def slot(g, t):
        return out_ref.at[g, t]

    def scatter(d):
        return remote(part_ref.at[far[d]], land.at[d], s1.at[d], r1.at[d], tile=far[d])

    def gather(d):
        return remote(slot(group, tile), slot(group, tile), s2.at[d], r2.at[d], tile=far[d])

    def held(d):
        return (tile - d + tiles) % tiles

    def over(d, i):
        place = slot(group, held(d))
        return remote(place, place, s3.at[d, i], r3.at[d, i], tm=others[i])

    def to_mate(d, i):
        place = slot(((chip - i + chips) % chips) * 2 + core, held(d))
        return remote(place, place, s4.at[d, i], r4.at[d, i], tm=mate)

    for d in range(tiles - 1):
        scatter(d).start()
    total = part_ref[tile]
    for d in range(tiles - 1):
        scatter(d).wait_recv()
        total = total + land[d]
    out_ref[group, tile] = total
    for d in range(tiles - 1):
        gather(d).start()
    for d in range(tiles):
        if d:
            gather(d - 1).wait_recv()
        for i in range(chips - 1):
            over(d, i).start()
        to_mate(d, 0).start()
    for d in range(tiles):
        for i in range(chips - 1):
            over(d, i).wait_recv()
            to_mate(d, i + 1).start()
    for d in range(tiles):
        for i in range(chips):
            to_mate(d, i).wait_recv()
            to_mate(d, i).wait_send()
        for i in range(chips - 1):
            over(d, i).wait_send()
    for d in range(tiles - 1):
        scatter(d).wait_send()
        gather(d).wait_send()


def stencil_kernel(
    tiles, block, basis_ref, d_ref, dx_ref, dy_ref, sea_ref, fringe_ref, halo_ref, info_ref, part_ref,
    prop_ref, turned, gf, gl, f1, l1, f2, l2, fh, fl, lh, ll
):
    width, rows, columns = basis_ref.shape
    halves = block // 8
    column = lax.broadcasted_iota(jnp.int32, (8, columns), 1)

    def cell(ref, i, r):
        if r < 0:
            line = fringe_ref[r + HALF, i : i + 1, :]
        elif r >= rows:
            line = fringe_ref[r - rows + HALF, i : i + 1, :]
        else:
            line = ref[r : r + 1, :]
        return jnp.broadcast_to(line, (8, columns))

    for r in range(-HALF, rows + HALF):
        d, dx, dy, sea = (
            cell(ref, i, r) for i, ref in enumerate((d_ref, dx_ref, dy_ref, sea_ref))
        )
        center = sea * (1.0 - 4.0 * d)
        east = sea * (d * (1.0 - dx))
        west = sea * (d * (1.0 + dx))
        north = jnp.where(column == columns - 1, 0.0, sea * (d * (1.0 - dy)))
        south = jnp.where(column == 0, 0.0, sea * (d * (1.0 + dy)))
        at = r + HALF - 1
        if 0 <= at < rows + 2 * (HALF - 1):
            for i, gain in enumerate((center, east, west, north, south)):
                gf[i, at] = gain
            gl[0, at] = center
            gl[3, at] = pltpu.roll(south, columns - 1, 1)
            gl[4, at] = pltpu.roll(north, 1, 1)
        if 0 <= at - 1 < rows + 2 * (HALF - 1):
            gl[1, at - 1] = west
        if 0 <= at + 1 < rows + 2 * (HALF - 1):
            gl[2, at + 1] = east

    def rolled(x):
        return pltpu.roll(x, columns - 1, 1), pltpu.roll(x, 1, 1)

    def update(g, r, center, east, west, north, south):
        return (
            g[0, r] * center + g[1, r] * east + g[2, r] * west + g[3, r] * north + g[4, r] * south
        )

    def fields(kb, _):
        k = pl.multiple_of(kb * block, block)

        def load(r, h):
            if r < 0:
                return halo_ref[r + HALF, pl.ds(k + 8 * h, 8), :]
            if r >= rows:
                return halo_ref[r - rows + HALF, pl.ds(k + 8 * h, 8), :]
            return turned[r, h]

        for h in range(halves):
            turned[:, h] = jnp.swapaxes(basis_ref[pl.ds(k + 8 * h, 8)], 0, 1)
        edge = HALF - 1
        before = [load(-edge - 1, h) for h in range(halves)]
        here = [load(-edge, h) for h in range(halves)]
        for r in range(-edge, rows + edge):
            after = [load(r + 1, h) for h in range(halves)]
            for h in range(halves):
                north, south = rolled(here[h])
                f1[r + edge, h] = update(gf, r + edge, here[h], after[h], before[h], north, south)
                l1[r + edge, h] = update(gl, r + edge, here[h], after[h], before[h], north, south)
            before, here = here, after
        for g, s1, s2, high, low in ((gf, f1, f2, fh, fl), (gl, l1, l2, lh, ll)):
            src, dst = s1, s2
            for step in range(1, HALF):
                reach = HALF - 1 - step
                before = [src[edge - reach - 1, h] for h in range(halves)]
                here = [src[edge - reach, h] for h in range(halves)]
                for r in range(-reach, rows + reach):
                    after = [src[r + 1 + edge, h] for h in range(halves)]
                    new = []
                    for h in range(halves):
                        north, south = rolled(here[h])
                        new.append(update(g, r + edge, here[h], after[h], before[h], north, south))
                    if step < HALF - 1:
                        for h in range(halves):
                            dst[r + edge, h] = new[h]
                    else:
                        a, b = split(jnp.concatenate(new, axis=0))
                        high[r, pl.ds(k, block), :] = a
                        low[r, pl.ds(k, block), :] = b
                    before, here = here, after
                src, dst = dst, src
        return 0

    lax.fori_loop(0, width // block, fields, 0)
    prop_ref[...] = jnp.zeros_like(prop_ref)

    def row(r, _):
        prop_ref[...] += (
            dot16(lh[r], fh[r], NT) + dot16(lh[r], fl[r], NT) + dot16(ll[r], fh[r], NT)
        )
        return 0

    lax.fori_loop(0, rows, row, 0)
    lines = width // tiles
    for n in range(tiles):
        part_ref[n, :lines, :] = prop_ref[n * lines : (n + 1) * lines, :]
        part_ref[n, lines : 2 * lines, :] = info_ref[n * lines : (n + 1) * lines, :]
        part_ref[n, 2 * lines :, :] = info_ref[width:, :]


def eye_of(n):
    i = lax.broadcasted_iota(jnp.int32, (n, n), 0)
    j = lax.broadcasted_iota(jnp.int32, (n, n), 1)
    return (i == j).astype(jnp.float32)


def invert(mats, invs, tmps):
    n = mats[0].shape[0]
    eye = eye_of(n)
    size = 0.0
    for a, x, t in zip(mats, invs, tmps):
        scale = 1.0 / jnp.max(jnp.sum(jnp.abs(a[...]), axis=0, keepdims=True))
        r = eye - scale * a[...]
        t[...] = r
        x[...] = scale * (eye + r)
        size = jnp.maximum(size, jnp.sum(r * r))

    def small(c):
        return jnp.logical_not(c[1] <= 1e-2) & (c[0] < 30)

    def grow(carry):
        it, _ = carry
        size = 0.0
        for x, t in zip(invs, tmps):
            r = t[...].astype(jnp.bfloat16)
            r = dot16(r, r, NN)
            t[...] = r
            x[...] += dot16(x[...].astype(jnp.bfloat16), r.astype(jnp.bfloat16), NN)
            size = jnp.maximum(size, jnp.sum(r * r))
        return it + 1, size

    lax.while_loop(small, grow, (0, size))

    def residual():
        size = 0.0
        for a, x, t in zip(mats, invs, tmps):
            r = eye - dot3(a[...], x[...])
            t[...] = r
            size = jnp.maximum(size, jnp.sum(r * r))
        return size

    def grow_exact(carry):
        it, _ = carry
        size = 0.0
        for x, t in zip(invs, tmps):
            r = dot32(t[...], t[...])
            t[...] = r
            x[...] += dot32(x[...], r)
            size = jnp.maximum(size, jnp.sum(r * r))
        return it + 1, size

    def again(_):
        size = 0.0
        for a, x, t in zip(mats, invs, tmps):
            scale = 1.0 / jnp.max(jnp.sum(jnp.abs(a[...]), axis=0, keepdims=True))
            r = eye - scale * a[...]
            t[...] = r
            x[...] = scale * (eye + r)
            size = jnp.maximum(size, jnp.sum(r * r))
        lax.while_loop(small, grow_exact, (0, size))
        return residual()

    size = residual()
    size = lax.cond(size <= 0.25, lambda v: v, again, size)

    def correct(carry):
        it, _ = carry
        for x, t in zip(invs, tmps):
            x[...] += dot3(x[...], t[...])
        return it + 1, residual()

    lax.while_loop(lambda c: (c[1] > 1e-6) & (c[0] < 6), correct, (0, size))
    for x, t in zip(invs, tmps):
        x[...] += dot3(x[...], t[...])


def join_kernel(groups, scale_prop, scale_obs, sums_ref, out_ref, s, x, t, w):
    n = sums_ref.shape[3]
    lines = n // sums_ref.shape[1]
    middle = groups // 2
    q = q_inverse
    eye = eye_of(n)

    def prop(g):
        return sums_ref[g, :, :lines, :].reshape(n, n) * scale_prop

    def diagonal(i):
        value = ridge * eye
        if i < groups:
            p = prop(i)
            value = value + q * dot32(p, p, TN)
        if i > 0:
            value = value + (q * eye + sums_ref[i - 1, :, lines : 2 * lines, :].reshape(n, n) * scale_obs)
            if i < groups:
                value = value + ridge * eye
        return value

    def right(i):
        if i == 0:
            return jnp.zeros((8, n), jnp.float32)
        return sums_ref[i - 1, 0, 2 * lines :, :] * scale_obs

    for i in range(groups + 1):
        s[i] = diagonal(i)
    vec = [right(i) for i in range(groups + 1)]
    for level in range(max(middle, groups - middle)):
        top = level if level < middle else None
        low = groups - level if groups - level > middle else None
        todo = [i for i in (top, low) if i is not None]
        invert([s.at[i] for i in todo], [x.at[i] for i in todo], [t.at[i] for i in todo])
        for i in todo:
            if i == top:
                p = prop(i)
                w[i] = q * dot3(x[i], p, NT)
                s[i + 1] -= q * dot32(p, w[i])
                vec[i + 1] = vec[i + 1] + dot32(vec[i], w[i])
            else:
                p = prop(i - 1)
                w[i] = q * dot3(x[i], p)
                s[i - 1] -= q * dot32(p, w[i], TN)
                vec[i - 1] = vec[i - 1] + dot32(vec[i], w[i])
    invert([s.at[middle]], [x.at[middle]], [t.at[middle]])
    state = {middle: dot32(vec[middle], x[middle])}
    for i in range(middle - 1, -1, -1):
        state[i] = dot32(vec[i], x[i]) + dot32(state[i + 1], w[i], NT)
    for i in range(middle + 1, groups + 1):
        state[i] = dot32(vec[i], x[i]) + dot32(state[i - 1], w[i], NT)
    for i in range(groups + 1):
        out_ref[i : i + 1, :] = state[i][:1]


VMEM = pltpu.VMEM


def shards(basis, diffusion, drift_x, drift_y, land_sea, obs_cells, obs_values):
    width, rows, columns = basis.shape
    nobs = obs_cells.shape[1]
    groups = lax.axis_size("tm")
    tiles = lax.axis_size("tile")
    group = lax.axis_index("tm")

    chips = groups // 2
    cells = (diffusion[0], drift_x[0], drift_y[0], land_sea.astype(jnp.float32))
    offset = lax.axis_index("tile") * (rows * columns)
    local = obs_cells[0] - offset
    inside = (local >= 0) & (local < rows * columns)
    row_of = jnp.where(inside, local // columns, -1)
    col_of = local % columns
    in_row = lax.broadcasted_iota(jnp.int32, (rows, nobs), 0) == row_of[None, :]
    in_col = (lax.broadcasted_iota(jnp.int32, (columns, nobs), 0) == col_of[None, :]).astype(
        jnp.float32
    )
    hits = jnp.concatenate(
        [in_row.astype(jnp.float32), jnp.where(in_row, obs_values[0][None, :], 0.0)], axis=0
    )
    hits = dot32(hits, in_col, NT)

    share = width // groups
    DMA = pltpu.SemaphoreType.DMA
    whole = pl.BlockSpec(memory_space=VMEM)
    halo, fringe, info = pl.pallas_call(
        functools.partial(edge_kernel, chips, tiles),
        out_shape=(
            jax.ShapeDtypeStruct((2 * HALF, width, columns), jnp.float32),
            jax.ShapeDtypeStruct((2 * HALF, 8, columns), jnp.float32),
            jax.ShapeDtypeStruct((width + 8, width), jnp.float32),
        ),
        in_specs=[whole] * 7,
        out_specs=[whole] * 3,
        scratch_shapes=[VMEM((2 * HALF, share, columns), jnp.float32)]
        + [VMEM((2 * HALF, 8, columns), jnp.float32)]
        + [VMEM((width, 128), jnp.float32)]
        + [VMEM((rows, width, columns), jnp.bfloat16)] * 2
        + [DMA((2,))] * 4
        + [DMA((2, max(chips - 1, 1)))] * 2
        + [DMA((2, chips))] * 2,
        compiler_params=pltpu.CompilerParams(
            vmem_limit_bytes=40 << 20, collective_id=0, has_side_effects=True
        ),
        name="edges",
    )(basis, *cells, hits[:rows], hits[rows:])
    block = 16
    edge_rows = rows + 2 * (HALF - 1)
    lines = 2 * width // tiles + 8
    part = pl.pallas_call(
        functools.partial(stencil_kernel, tiles, block),
        out_shape=jax.ShapeDtypeStruct((tiles, lines, width), jnp.float32),
        in_specs=[whole] * 8,
        out_specs=pl.BlockSpec(memory_space=VMEM),
        scratch_shapes=[VMEM((width, width), jnp.float32)]
        + [VMEM((rows, block // 8, 8, columns), jnp.float32)]
        + [VMEM((5, edge_rows, 8, columns), jnp.float32)] * 2
        + [VMEM((edge_rows, block // 8, 8, columns), jnp.float32)] * 4
        + [VMEM((rows, width, columns), jnp.bfloat16)] * 4,
        compiler_params=pltpu.CompilerParams(vmem_limit_bytes=48 << 20),
        cost_estimate=pl.CostEstimate(
            flops=20000 * width * rows * columns,
            bytes_accessed=4 * width * rows * columns,
            transcendentals=0,
        ),
        name="propagate",
    )(basis, *cells, fringe, halo, info)

    sums = pl.pallas_call(
        functools.partial(spread_kernel, chips, tiles),
        out_shape=jax.ShapeDtypeStruct((groups, tiles, lines, width), jnp.float32),
        in_specs=[whole],
        out_specs=whole,
        scratch_shapes=[VMEM((tiles - 1, lines, width), jnp.float32)]
        + [DMA((tiles - 1,))] * 4
        + [DMA((tiles, max(chips - 1, 1)))] * 2
        + [DMA((tiles, chips))] * 2,
        compiler_params=pltpu.CompilerParams(
            vmem_limit_bytes=16 << 20, collective_id=1, has_side_effects=True
        ),
        name="spread",
    )(part)
    states = pl.pallas_call(
        functools.partial(
            join_kernel, groups, 1.0 / (rows * columns * tiles), 1.0 / nobs
        ),
        out_shape=jax.ShapeDtypeStruct((groups + 1, width), jnp.float32),
        in_specs=[whole],
        out_specs=whole,
        scratch_shapes=[VMEM((groups + 1, width, width), jnp.float32)] * 4,
        compiler_params=pltpu.CompilerParams(vmem_limit_bytes=48 << 20),
        name="join",
    )(sums)
    coeffs = lax.dynamic_slice_in_dim(states, group, 2, axis=0)
    end_fields = jnp.sum(coeffs[1][:, None, None] * basis, axis=0)
    return coeffs[None], end_fields[None]


def solution(mesh):
    in_specs = (
        P(None, "tile", None),
        P("tm", "tile", None),
        P("tm", "tile", None),
        P("tm", "tile", None),
        P("tile", None),
        P("tm", None),
        P("tm", None),
    )
    out_specs = (P("tm", None, None), P("tm", "tile", None))
    return jax.shard_map(shards, mesh=mesh, in_specs=in_specs, out_specs=out_specs, check_vma=False)
```

```python
import functools

import jax
import jax.numpy as jnp
from jax import lax
from jax.experimental import pallas as pl
from jax.experimental.pallas import tpu as pltpu
from jax.sharding import PartitionSpec as P

STEPS = 6
HALF = STEPS // 2
CHUNKS = 4

q_inverse = 10.0
ridge = 0.1

NT = (((1,), (1,)), ((), ()))
NN = (((1,), (0,)), ((), ()))
TN = (((0,), (0,)), ((), ()))


def split(x):
    high = x.astype(jnp.bfloat16)
    return high, (x - high.astype(jnp.float32)).astype(jnp.bfloat16)


def dot16(a, b, dims):
    return lax.dot_general(a, b, dims, preferred_element_type=jnp.float32)


def dot32(a, b, dims=NN):
    return lax.dot_general(
        a, b, dims, precision=lax.Precision.HIGHEST, preferred_element_type=jnp.float32
    )


def dot3(a, b, dims=NN):
    ah, al = split(a)
    bh, bl = split(b)
    return dot16(ah, bh, dims) + dot16(ah, bl, dims) + dot16(al, bh, dims)


MESH = pl.DeviceIdType.MESH


def remote(src, dst, send, recv, **where):
    return pltpu.make_async_remote_copy(
        src_ref=src, dst_ref=dst, send_sem=send, recv_sem=recv, device_id=where, device_id_type=MESH
    )


def edge_kernel(
    chips, tiles, basis_ref, d_ref, dx_ref, dy_ref, sea_ref, where_ref, value_ref, halo_ref, fringe_ref, info_ref,
    edge, cells_ref, hits_ref, rhs_ref, xh, xl, first_send, first_recv, cell_send, cell_recv, over_send, over_recv,
    mate_send, mate_recv,
):
    width, rows, columns = basis_ref.shape
    group, tile = lax.axis_index("tm"), lax.axis_index("tile")
    chip, core = group // 2, group % 2
    mate = group + 1 - 2 * core
    share = edge.shape[1]
    piece = share // CHUNKS
    mine = pl.multiple_of(group * share, share)
    others = [((chip + i) % chips) * 2 + core for i in range(1, chips)]
    has = (tile > 0, tile < tiles - 1)
    near = (tile - 1, tile + 1)

    barrier = pltpu.get_barrier_semaphore()
    for peer in others + [mate]:
        pl.semaphore_signal(barrier, inc=1, device_id={"tm": peer}, device_id_type=MESH)
    for peer in ((tile + tiles - 1) % tiles, (tile + 1) % tiles):
        pl.semaphore_signal(barrier, inc=1, device_id={"tile": peer}, device_id_type=MESH)

    cells_ref[...] = jnp.zeros_like(cells_ref)
    for i, ref in enumerate((d_ref, dx_ref, dy_ref, sea_ref)):
        for r in range(HALF):
            cells_ref[r, i : i + 1, :] = ref[r : r + 1, :].astype(jnp.float32)
            last = rows - HALF + r
            cells_ref[HALF + r, i : i + 1, :] = ref[last : last + 1, :].astype(jnp.float32)

    def cut(j, _):
        x = basis_ref[pl.ds(mine + 8 * j, 8)]
        y = jnp.swapaxes(x, 0, 1)
        k = pl.multiple_of(8 * j, 8)
        edge[:HALF, pl.ds(k, 8), :] = y[:HALF]
        edge[HALF:, pl.ds(k, 8), :] = y[rows - HALF :]
        return 0

    lax.fori_loop(0, share // 8, cut, 0)
    pl.semaphore_wait(barrier, chips + 2)

    def part(side, g, j):
        k = pl.multiple_of(g * share + j * piece, piece)
        return halo_ref.at[pl.ds(side * HALF, HALF), pl.ds(k, piece), :]

    def ours(side, j):
        return edge.at[pl.ds(side * HALF, HALF), pl.ds(j * piece, piece), :]

    def send(side, j):
        other = 1 - side
        return remote(ours(side, j), part(other, group, j), first_send.at[side, j],
                      first_recv.at[other, j], tile=near[side])

    def arrival(side, j):
        return remote(ours(side, j), part(side, group, j), first_send.at[side, j],
                      first_recv.at[side, j], tile=near[side])

    def send_cells(side):
        other = 1 - side
        return remote(cells_ref.at[pl.ds(side * HALF, HALF)],
                      fringe_ref.at[pl.ds(other * HALF, HALF)],
                      cell_send.at[side], cell_recv.at[other], tile=near[side])

    def cells_arrival(side):
        return remote(cells_ref.at[pl.ds(side * HALF, HALF)],
                      fringe_ref.at[pl.ds(side * HALF, HALF)],
                      cell_send.at[side], cell_recv.at[side], tile=near[side])

    def over(side, j, i):
        place = part(side, group, j)
        return remote(place, place, over_send.at[side, j, i], over_recv.at[side, j, i],
                      tm=others[i])

    def to_mate(side, j, i):
        place = part(side, ((chip - i + chips) % chips) * 2 + core, j)
        return remote(place, place, mate_send.at[side, j, i], mate_recv.at[side, j, i], tm=mate)

    for j in range(CHUNKS):
        for side in range(2):

            @pl.when(has[side])
            def _():
                send(side, j).start()

    for side in range(2):

        @pl.when(has[side])
        def _():
            send_cells(side).start()

        @pl.when(jnp.logical_not(has[side]))
        def _():
            halo_ref[side * HALF : (side + 1) * HALF] = jnp.zeros(
                (HALF, width, columns), jnp.float32
            )
            fringe_ref[side * HALF : (side + 1) * HALF] = jnp.zeros(
                (HALF,) + fringe_ref.shape[1:], jnp.float32
            )

    nobs = where_ref.shape[1]
    local = where_ref[...] - tile * (rows * columns)
    first = lax.broadcasted_iota(jnp.int32, (rows, nobs), 0) * columns
    in_row = (local >= first) & (local < first + columns)
    col_of = local - jnp.sum(jnp.where(in_row, first, 0), axis=0, keepdims=True)
    in_col = (lax.broadcasted_iota(jnp.int32, (columns, nobs), 0) == col_of).astype(jnp.float32)
    hits_ref[:rows, :] = dot32(in_row.astype(jnp.float32), in_col, NT)
    hits_ref[rows:, :] = dot32(jnp.where(in_row, value_ref[...], 0.0), in_col, NT)

    def turn(j, _):
        k = pl.multiple_of(16 * j, 16)
        y = jnp.swapaxes(basis_ref[pl.ds(k, 16)], 0, 1)
        high, low = split(y)
        xh[:, pl.ds(k, 16), :] = high
        xl[:, pl.ds(k, 16), :] = low
        return 0

    lax.fori_loop(0, width // 16, turn, 0)
    info_ref[...] = jnp.zeros_like(info_ref)
    rhs_ref[...] = jnp.zeros_like(rhs_ref)

    def row(r, _):
        a, b = xh[r], xl[r]
        x = a.astype(jnp.float32) + b.astype(jnp.float32)
        yh, yl = split(x * hits_ref[pl.ds(r, 1), :])
        z = x * hits_ref[pl.ds(rows + r, 1), :]
        info_ref[:width, :] += dot16(a, yh, NT) + dot16(a, yl, NT) + dot16(b, yh, NT)
        part_sum = z[:, :128]
        for c in range(128, columns, 128):
            part_sum += z[:, c : c + 128]
        rhs_ref[...] += part_sum
        return 0

    for j in range(CHUNKS):
        lax.fori_loop(j * rows // CHUNKS, (j + 1) * rows // CHUNKS, row, 0)
        for side in range(2):

            @pl.when(has[side])
            def _():
                arrival(side, j).wait_recv()
                for i in range(chips - 1):
                    over(side, j, i).start()
                to_mate(side, j, 0).start()
                if j:
                    for i in range(chips - 1):
                        over(side, j - 1, i).wait_recv()
                        to_mate(side, j - 1, i + 1).start()

    for side in range(2):

        @pl.when(has[side])
        def _():
            for i in range(chips - 1):
                over(side, CHUNKS - 1, i).wait_recv()
                to_mate(side, CHUNKS - 1, i + 1).start()

    for side in range(2):

        @pl.when(has[side])
        def _():
            for j in range(CHUNKS):
                for i in range(chips):
                    to_mate(side, j, i).wait_recv()
                    to_mate(side, j, i).wait_send()
                for i in range(chips - 1):
                    over(side, j, i).wait_send()
                send(side, j).wait_send()
            cells_arrival(side).wait_recv()
            send_cells(side).wait_send()

    info_ref[width:, :] = dot32(jnp.ones((8, 128), jnp.float32), rhs_ref[...], NT)


def spread_kernel(chips, tiles, part_ref, out_ref, land, s1, r1, s2, r2, s3, r3, s4, r4):
    group, tile = lax.axis_index("tm"), lax.axis_index("tile")
    chip, core = group // 2, group % 2
    mate = group + 1 - 2 * core
    others = [((chip + i) % chips) * 2 + core for i in range(1, chips)]
    far = [(tile + d) % tiles for d in range(1, tiles)]

    barrier = pltpu.get_barrier_semaphore()
    for peer in others + [mate]:
        pl.semaphore_signal(barrier, inc=1, device_id={"tm": peer}, device_id_type=MESH)
    for peer in far:
        pl.semaphore_signal(barrier, inc=1, device_id={"tile": peer}, device_id_type=MESH)
    pl.semaphore_wait(barrier, chips + tiles - 1)

    def slot(g, t):
        return out_ref.at[g, t]

    def scatter(d):
        return remote(part_ref.at[far[d]], land.at[d], s1.at[d], r1.at[d], tile=far[d])

    def gather(d):
        return remote(slot(group, tile), slot(group, tile), s2.at[d], r2.at[d], tile=far[d])

    def held(d):
        return (tile - d + tiles) % tiles

    def over(d, i):
        place = slot(group, held(d))
        return remote(place, place, s3.at[d, i], r3.at[d, i], tm=others[i])

    def to_mate(d, i):
        place = slot(((chip - i + chips) % chips) * 2 + core, held(d))
        return remote(place, place, s4.at[d, i], r4.at[d, i], tm=mate)

    for d in range(tiles - 1):
        scatter(d).start()
    total = part_ref[tile]
    for d in range(tiles - 1):
        scatter(d).wait_recv()
        total = total + land[d]
    out_ref[group, tile] = total
    for d in range(tiles - 1):
        gather(d).start()
    for d in range(tiles):
        if d:
            gather(d - 1).wait_recv()
        for i in range(chips - 1):
            over(d, i).start()
        to_mate(d, 0).start()
    for d in range(tiles):
        for i in range(chips - 1):
            over(d, i).wait_recv()
            to_mate(d, i + 1).start()
    for d in range(tiles):
        for i in range(chips):
            to_mate(d, i).wait_recv()
            to_mate(d, i).wait_send()
        for i in range(chips - 1):
            over(d, i).wait_send()
    for d in range(tiles - 1):
        scatter(d).wait_send()
        gather(d).wait_send()


def stencil_kernel(
    tiles, block, basis_ref, d_ref, dx_ref, dy_ref, sea_ref, fringe_ref, halo_ref, info_ref, part_ref,
    prop_ref, turned, gf, gl, f1, l1, f2, l2, fh, fl, lh, ll
):
    width, rows, columns = basis_ref.shape
    halves = block // 8
    column = lax.broadcasted_iota(jnp.int32, (8, columns), 1)

    def cell(ref, i, r):
        if r < 0:
            line = fringe_ref[r + HALF, i : i + 1, :]
        elif r >= rows:
            line = fringe_ref[r - rows + HALF, i : i + 1, :]
        else:
            line = ref[r : r + 1, :]
        return jnp.broadcast_to(line.astype(jnp.float32), (8, columns))

    for r in range(-HALF, rows + HALF):
        d, dx, dy, sea = (
            cell(ref, i, r) for i, ref in enumerate((d_ref, dx_ref, dy_ref, sea_ref))
        )
        center = sea * (1.0 - 4.0 * d)
        east = sea * (d * (1.0 - dx))
        west = sea * (d * (1.0 + dx))
        north = jnp.where(column == columns - 1, 0.0, sea * (d * (1.0 - dy)))
        south = jnp.where(column == 0, 0.0, sea * (d * (1.0 + dy)))
        at = r + HALF - 1
        if 0 <= at < rows + 2 * (HALF - 1):
            for i, gain in enumerate((center, east, west, north, south)):
                gf[i, at] = gain
            gl[0, at] = center
            gl[3, at] = pltpu.roll(south, columns - 1, 1)
            gl[4, at] = pltpu.roll(north, 1, 1)
        if 0 <= at - 1 < rows + 2 * (HALF - 1):
            gl[1, at - 1] = west
        if 0 <= at + 1 < rows + 2 * (HALF - 1):
            gl[2, at + 1] = east

    def rolled(x):
        return pltpu.roll(x, columns - 1, 1), pltpu.roll(x, 1, 1)

    def update(g, r, center, east, west, north, south):
        return (
            g[0, r] * center + g[1, r] * east + g[2, r] * west + g[3, r] * north + g[4, r] * south
        )

    def fields(kb, _):
        k = pl.multiple_of(kb * block, block)

        def load(r, h):
            if r < 0:
                return halo_ref[r + HALF, pl.ds(k + 8 * h, 8), :]
            if r >= rows:
                return halo_ref[r - rows + HALF, pl.ds(k + 8 * h, 8), :]
            return turned[r, h]

        for h in range(halves):
            turned[:, h] = jnp.swapaxes(basis_ref[pl.ds(k + 8 * h, 8)], 0, 1)
        edge = HALF - 1
        before = [load(-edge - 1, h) for h in range(halves)]
        here = [load(-edge, h) for h in range(halves)]
        for r in range(-edge, rows + edge):
            after = [load(r + 1, h) for h in range(halves)]
            for h in range(halves):
                north, south = rolled(here[h])
                f1[r + edge, h] = update(gf, r + edge, here[h], after[h], before[h], north, south)
                l1[r + edge, h] = update(gl, r + edge, here[h], after[h], before[h], north, south)
            before, here = here, after
        for g, s1, s2, high, low in ((gf, f1, f2, fh, fl), (gl, l1, l2, lh, ll)):
            src, dst = s1, s2
            for step in range(1, HALF):
                reach = HALF - 1 - step
                before = [src[edge - reach - 1, h] for h in range(halves)]
                here = [src[edge - reach, h] for h in range(halves)]
                for r in range(-reach, rows + reach):
                    after = [src[r + 1 + edge, h] for h in range(halves)]
                    new = []
                    for h in range(halves):
                        north, south = rolled(here[h])
                        new.append(update(g, r + edge, here[h], after[h], before[h], north, south))
                    if step < HALF - 1:
                        for h in range(halves):
                            dst[r + edge, h] = new[h]
                    else:
                        a, b = split(jnp.concatenate(new, axis=0))
                        high[r, pl.ds(k, block), :] = a
                        low[r, pl.ds(k, block), :] = b
                    before, here = here, after
                src, dst = dst, src
        return 0

    lax.fori_loop(0, width // block, fields, 0)
    prop_ref[...] = jnp.zeros_like(prop_ref)

    def row(r, _):
        prop_ref[...] += (
            dot16(lh[r], fh[r], NT) + dot16(lh[r], fl[r], NT) + dot16(ll[r], fh[r], NT)
        )
        return 0

    lax.fori_loop(0, rows, row, 0)
    lines = width // tiles
    for n in range(tiles):
        part_ref[n, :lines, :] = prop_ref[n * lines : (n + 1) * lines, :]
        part_ref[n, lines : 2 * lines, :] = info_ref[n * lines : (n + 1) * lines, :]
        part_ref[n, 2 * lines :, :] = info_ref[width:, :]


def eye_of(n):
    i = lax.broadcasted_iota(jnp.int32, (n, n), 0)
    j = lax.broadcasted_iota(jnp.int32, (n, n), 1)
    return (i == j).astype(jnp.float32)


def invert(mats, invs, tmps):
    n = mats[0].shape[0]
    eye = eye_of(n)
    size = 0.0
    for a, x, t in zip(mats, invs, tmps):
        scale = 1.0 / jnp.max(jnp.sum(jnp.abs(a[...]), axis=0, keepdims=True))
        r = eye - scale * a[...]
        t[...] = r
        x[...] = scale * (eye + r)
        size = jnp.maximum(size, jnp.sum(r * r))

    def small(c):
        return jnp.logical_not(c[1] <= 1e-2) & (c[0] < 30)

    def grow(carry):
        it, _ = carry
        size = 0.0
        for x, t in zip(invs, tmps):
            r = t[...].astype(jnp.bfloat16)
            r = dot16(r, r, NN)
            t[...] = r
            x[...] += dot16(x[...].astype(jnp.bfloat16), r.astype(jnp.bfloat16), NN)
            size = jnp.maximum(size, jnp.sum(r * r))
        return it + 1, size

    lax.while_loop(small, grow, (0, size))

    def residual():
        size = 0.0
        for a, x, t in zip(mats, invs, tmps):
            r = eye - dot3(a[...], x[...])
            t[...] = r
            size = jnp.maximum(size, jnp.sum(r * r))
        return size

    def grow_exact(carry):
        it, _ = carry
        size = 0.0
        for x, t in zip(invs, tmps):
            r = dot32(t[...], t[...])
            t[...] = r
            x[...] += dot32(x[...], r)
            size = jnp.maximum(size, jnp.sum(r * r))
        return it + 1, size

    def again(_):
        size = 0.0
        for a, x, t in zip(mats, invs, tmps):
            scale = 1.0 / jnp.max(jnp.sum(jnp.abs(a[...]), axis=0, keepdims=True))
            r = eye - scale * a[...]
            t[...] = r
            x[...] = scale * (eye + r)
            size = jnp.maximum(size, jnp.sum(r * r))
        lax.while_loop(small, grow_exact, (0, size))
        return residual()

    size = residual()
    size = lax.cond(size <= 0.25, lambda v: v, again, size)

    def correct(carry):
        it, _ = carry
        for x, t in zip(invs, tmps):
            x[...] += dot3(x[...], t[...])
        return it + 1, residual()

    lax.while_loop(lambda c: (c[1] > 1e-6) & (c[0] < 6), correct, (0, size))
    for x, t in zip(invs, tmps):
        x[...] += dot3(x[...], t[...])


def join_kernel(
    groups, scale_prop, scale_obs, sums_ref, basis_ref, coeff_ref, field_ref, s, x, t, w, st, col
):
    n = sums_ref.shape[3]
    lines = n // sums_ref.shape[1]
    middle = groups // 2
    q = q_inverse
    eye = eye_of(n)

    def prop(g):
        return sums_ref[g, :, :lines, :].reshape(n, n) * scale_prop

    def diagonal(i):
        value = ridge * eye
        if i < groups:
            p = prop(i)
            value = value + q * dot32(p, p, TN)
        if i > 0:
            value = value + (q * eye + sums_ref[i - 1, :, lines : 2 * lines, :].reshape(n, n) * scale_obs)
            if i < groups:
                value = value + ridge * eye
        return value

    def right(i):
        if i == 0:
            return jnp.zeros((8, n), jnp.float32)
        return sums_ref[i - 1, 0, 2 * lines :, :] * scale_obs

    for i in range(groups + 1):
        s[i] = diagonal(i)
    vec = [right(i) for i in range(groups + 1)]
    for level in range(max(middle, groups - middle)):
        top = level if level < middle else None
        low = groups - level if groups - level > middle else None
        todo = [i for i in (top, low) if i is not None]
        invert([s.at[i] for i in todo], [x.at[i] for i in todo], [t.at[i] for i in todo])
        for i in todo:
            if i == top:
                p = prop(i)
                w[i] = q * dot3(x[i], p, NT)
                s[i + 1] -= q * dot32(p, w[i])
                vec[i + 1] = vec[i + 1] + dot32(vec[i], w[i])
            else:
                p = prop(i - 1)
                w[i] = q * dot3(x[i], p)
                s[i - 1] -= q * dot32(p, w[i], TN)
                vec[i - 1] = vec[i - 1] + dot32(vec[i], w[i])
    invert([s.at[middle]], [x.at[middle]], [t.at[middle]])
    state = {middle: dot32(vec[middle], x[middle])}
    for i in range(middle - 1, -1, -1):
        state[i] = dot32(vec[i], x[i]) + dot32(state[i + 1], w[i], NT)
    for i in range(middle + 1, groups + 1):
        state[i] = dot32(vec[i], x[i]) + dot32(state[i - 1], w[i], NT)
    for i in range(groups + 1):
        st[i] = state[i]
    group = lax.axis_index("tm")
    coeff_ref[0:1, :] = st[group][:1]
    end = st[group + 1]
    coeff_ref[1:2, :] = end[:1]
    col[...] = dot32(eye, end, NT)

    def add(j, total):
        k = pl.multiple_of(8 * j, 8)
        weights = col[pl.ds(k, 8), :]
        for i in range(8):
            total = total + weights[i : i + 1, 0:1] * basis_ref[k + i]
        return total

    field_ref[...] = lax.fori_loop(0, n // 8, add, jnp.zeros(field_ref.shape, jnp.float32))


VMEM = pltpu.VMEM


def shards(basis, diffusion, drift_x, drift_y, land_sea, obs_cells, obs_values):
    width, rows, columns = basis.shape
    nobs = obs_cells.shape[1]
    groups = lax.axis_size("tm")
    tiles = lax.axis_size("tile")
    chips = groups // 2
    cells = (diffusion[0], drift_x[0], drift_y[0], land_sea)
    share = width // groups
    DMA = pltpu.SemaphoreType.DMA
    whole = pl.BlockSpec(memory_space=VMEM)
    halo, fringe, info = pl.pallas_call(
        functools.partial(edge_kernel, chips, tiles),
        out_shape=(
            jax.ShapeDtypeStruct((2 * HALF, width, columns), jnp.float32),
            jax.ShapeDtypeStruct((2 * HALF, 8, columns), jnp.float32),
            jax.ShapeDtypeStruct((width + 8, width), jnp.float32),
        ),
        in_specs=[whole] * 7,
        out_specs=[whole] * 3,
        scratch_shapes=[VMEM((2 * HALF, share, columns), jnp.float32)]
        + [VMEM((2 * HALF, 8, columns), jnp.float32)]
        + [VMEM((2 * rows, columns), jnp.float32)]
        + [VMEM((width, 128), jnp.float32)]
        + [VMEM((rows, width, columns), jnp.bfloat16)] * 2
        + [DMA((2, CHUNKS))] * 2
        + [DMA((2,))] * 2
        + [DMA((2, CHUNKS, max(chips - 1, 1)))] * 2
        + [DMA((2, CHUNKS, chips))] * 2,
        compiler_params=pltpu.CompilerParams(
            vmem_limit_bytes=40 << 20, collective_id=0, has_side_effects=True
        ),
        name="edges",
    )(basis, *cells, obs_cells, obs_values)
    block = 16
    edge_rows = rows + 2 * (HALF - 1)
    lines = 2 * width // tiles + 8
    part = pl.pallas_call(
        functools.partial(stencil_kernel, tiles, block),
        out_shape=jax.ShapeDtypeStruct((tiles, lines, width), jnp.float32),
        in_specs=[whole] * 8,
        out_specs=pl.BlockSpec(memory_space=VMEM),
        scratch_shapes=[VMEM((width, width), jnp.float32)]
        + [VMEM((rows, block // 8, 8, columns), jnp.float32)]
        + [VMEM((5, edge_rows, 8, columns), jnp.float32)] * 2
        + [VMEM((edge_rows, block // 8, 8, columns), jnp.float32)] * 4
        + [VMEM((rows, width, columns), jnp.bfloat16)] * 4,
        compiler_params=pltpu.CompilerParams(vmem_limit_bytes=48 << 20),
        cost_estimate=pl.CostEstimate(
            flops=20000 * width * rows * columns,
            bytes_accessed=4 * width * rows * columns,
            transcendentals=0,
        ),
        name="propagate",
    )(basis, *cells, fringe, halo, info)

    sums = pl.pallas_call(
        functools.partial(spread_kernel, chips, tiles),
        out_shape=jax.ShapeDtypeStruct((groups, tiles, lines, width), jnp.float32),
        in_specs=[whole],
        out_specs=whole,
        scratch_shapes=[VMEM((tiles - 1, lines, width), jnp.float32)]
        + [DMA((tiles - 1,))] * 4
        + [DMA((tiles, max(chips - 1, 1)))] * 2
        + [DMA((tiles, chips))] * 2,
        compiler_params=pltpu.CompilerParams(
            vmem_limit_bytes=16 << 20, collective_id=1, has_side_effects=True
        ),
        name="spread",
    )(part)
    coeffs, end_fields = pl.pallas_call(
        functools.partial(
            join_kernel, groups, 1.0 / (rows * columns * tiles), 1.0 / nobs
        ),
        out_shape=(
            jax.ShapeDtypeStruct((2, width), jnp.float32),
            jax.ShapeDtypeStruct((rows, columns), jnp.float32),
        ),
        in_specs=[whole] * 2,
        out_specs=[whole] * 2,
        scratch_shapes=[VMEM((groups + 1, width, width), jnp.float32)] * 4
        + [VMEM((groups + 1, 8, width), jnp.float32), VMEM((width, 8), jnp.float32)],
        compiler_params=pltpu.CompilerParams(vmem_limit_bytes=40 << 20),
        name="join",
    )(sums, basis)
    return coeffs[None], end_fields[None]


def solution(mesh):
    in_specs = (
        P(None, "tile", None),
        P("tm", "tile", None),
        P("tm", "tile", None),
        P("tm", "tile", None),
        P("tile", None),
        P("tm", None),
        P("tm", None),
    )
    out_specs = (P("tm", None, None), P("tm", "tile", None))
    return jax.shard_map(shards, mesh=mesh, in_specs=in_specs, out_specs=out_specs, check_vma=False)
```

```python
import functools

import jax
import jax.numpy as jnp
from jax import lax
from jax.experimental import pallas as pl
from jax.experimental.pallas import tpu as pltpu
from jax.sharding import PartitionSpec as P

STEPS = 6
HALF = STEPS // 2
CHUNKS = 4

q_inverse = 10.0
ridge = 0.1

NT = (((1,), (1,)), ((), ()))
NN = (((1,), (0,)), ((), ()))
TN = (((0,), (0,)), ((), ()))


def split(x):
    high = x.astype(jnp.bfloat16)
    return high, (x - high.astype(jnp.float32)).astype(jnp.bfloat16)


def dot16(a, b, dims):
    return lax.dot_general(a, b, dims, preferred_element_type=jnp.float32)


def dot32(a, b, dims=NN):
    return lax.dot_general(
        a, b, dims, precision=lax.Precision.HIGHEST, preferred_element_type=jnp.float32
    )


def dot3(a, b, dims=NN):
    ah, al = split(a)
    bh, bl = split(b)
    return dot16(ah, bh, dims) + dot16(ah, bl, dims) + dot16(al, bh, dims)


MESH = pl.DeviceIdType.MESH


def remote(src, dst, send, recv, **where):
    return pltpu.make_async_remote_copy(
        src_ref=src, dst_ref=dst, send_sem=send, recv_sem=recv, device_id=where, device_id_type=MESH
    )


def edge_kernel(
    chips, tiles, basis_ref, d_ref, dx_ref, dy_ref, sea_ref, where_ref, value_ref, halo_ref, fringe_ref, info_ref,
    edge, cells_ref, hits_ref, rhs_ref, xh, xl, first_send, first_recv, cell_send, cell_recv, over_send, over_recv,
    mate_send, mate_recv,
):
    width, rows, columns = basis_ref.shape
    group, tile = lax.axis_index("tm"), lax.axis_index("tile")
    chip, core = group // 2, group % 2
    mate = group + 1 - 2 * core
    share = edge.shape[1]
    piece = share // CHUNKS
    mine = pl.multiple_of(group * share, share)
    others = [((chip + i) % chips) * 2 + core for i in range(1, chips)]
    has = (tile > 0, tile < tiles - 1)
    near = (tile - 1, tile + 1)

    barrier = pltpu.get_barrier_semaphore()
    for peer in others + [mate]:
        pl.semaphore_signal(barrier, inc=1, device_id={"tm": peer}, device_id_type=MESH)
    for peer in ((tile + tiles - 1) % tiles, (tile + 1) % tiles):
        pl.semaphore_signal(barrier, inc=1, device_id={"tile": peer}, device_id_type=MESH)

    cells_ref[...] = jnp.zeros_like(cells_ref)
    for i, ref in enumerate((d_ref, dx_ref, dy_ref, sea_ref)):
        for r in range(HALF):
            cells_ref[r, i : i + 1, :] = ref[r : r + 1, :].astype(jnp.float32)
            last = rows - HALF + r
            cells_ref[HALF + r, i : i + 1, :] = ref[last : last + 1, :].astype(jnp.float32)

    def cut(j, _):
        x = basis_ref[pl.ds(mine + 8 * j, 8)]
        y = jnp.swapaxes(x, 0, 1)
        k = pl.multiple_of(8 * j, 8)
        edge[:HALF, pl.ds(k, 8), :] = y[:HALF]
        edge[HALF:, pl.ds(k, 8), :] = y[rows - HALF :]
        return 0

    lax.fori_loop(0, share // 8, cut, 0)
    pl.semaphore_wait(barrier, chips + 2)

    def part(side, g, j):
        k = pl.multiple_of(g * share + j * piece, piece)
        return halo_ref.at[pl.ds(side * HALF, HALF), pl.ds(k, piece), :]

    def ours(side, j):
        return edge.at[pl.ds(side * HALF, HALF), pl.ds(j * piece, piece), :]

    def send(side, j):
        other = 1 - side
        return remote(ours(side, j), part(other, group, j), first_send.at[side, j],
                      first_recv.at[other, j], tile=near[side])

    def arrival(side, j):
        return remote(ours(side, j), part(side, group, j), first_send.at[side, j],
                      first_recv.at[side, j], tile=near[side])

    def send_cells(side):
        other = 1 - side
        return remote(cells_ref.at[pl.ds(side * HALF, HALF)],
                      fringe_ref.at[pl.ds(other * HALF, HALF)],
                      cell_send.at[side], cell_recv.at[other], tile=near[side])

    def cells_arrival(side):
        return remote(cells_ref.at[pl.ds(side * HALF, HALF)],
                      fringe_ref.at[pl.ds(side * HALF, HALF)],
                      cell_send.at[side], cell_recv.at[side], tile=near[side])

    def over(side, j, i):
        place = part(side, group, j)
        return remote(place, place, over_send.at[side, j, i], over_recv.at[side, j, i],
                      tm=others[i])

    def to_mate(side, j, i):
        place = part(side, ((chip - i + chips) % chips) * 2 + core, j)
        return remote(place, place, mate_send.at[side, j, i], mate_recv.at[side, j, i], tm=mate)

    for j in range(CHUNKS):
        for side in range(2):

            @pl.when(has[side])
            def _():
                send(side, j).start()

    for side in range(2):

        @pl.when(has[side])
        def _():
            send_cells(side).start()

        @pl.when(jnp.logical_not(has[side]))
        def _():
            halo_ref[side * HALF : (side + 1) * HALF] = jnp.zeros(
                (HALF, width, columns), jnp.float32
            )
            fringe_ref[side * HALF : (side + 1) * HALF] = jnp.zeros(
                (HALF,) + fringe_ref.shape[1:], jnp.float32
            )

    nobs = where_ref.shape[1]
    local = where_ref[...] - tile * (rows * columns)
    first = lax.broadcasted_iota(jnp.int32, (rows, nobs), 0) * columns
    in_row = (local >= first) & (local < first + columns)
    col_of = local - jnp.sum(jnp.where(in_row, first, 0), axis=0, keepdims=True)
    in_col = (lax.broadcasted_iota(jnp.int32, (columns, nobs), 0) == col_of).astype(jnp.float32)
    hits_ref[:rows, :] = dot32(in_row.astype(jnp.float32), in_col, NT)
    hits_ref[rows:, :] = dot32(jnp.where(in_row, value_ref[...], 0.0), in_col, NT)

    def turn(j, _):
        k = pl.multiple_of(16 * j, 16)
        y = jnp.swapaxes(basis_ref[pl.ds(k, 16)], 0, 1)
        high, low = split(y)
        xh[:, pl.ds(k, 16), :] = high
        xl[:, pl.ds(k, 16), :] = low
        return 0

    lax.fori_loop(0, width // 16, turn, 0)
    info_ref[...] = jnp.zeros_like(info_ref)
    rhs_ref[...] = jnp.zeros_like(rhs_ref)

    def row(r, _):
        a, b = xh[r], xl[r]
        x = a.astype(jnp.float32) + b.astype(jnp.float32)
        yh, yl = split(x * hits_ref[pl.ds(r, 1), :])
        z = x * hits_ref[pl.ds(rows + r, 1), :]
        info_ref[:width, :] += dot16(a, yh, NT) + dot16(a, yl, NT) + dot16(b, yh, NT)
        part_sum = z[:, :128]
        for c in range(128, columns, 128):
            part_sum += z[:, c : c + 128]
        rhs_ref[...] += part_sum
        return 0

    for j in range(CHUNKS):
        lax.fori_loop(j * rows // CHUNKS, (j + 1) * rows // CHUNKS, row, 0)
        for side in range(2):

            @pl.when(has[side])
            def _():
                arrival(side, j).wait_recv()
                for i in range(chips - 1):
                    over(side, j, i).start()
                to_mate(side, j, 0).start()
                if j:
                    for i in range(chips - 1):
                        over(side, j - 1, i).wait_recv()
                        to_mate(side, j - 1, i + 1).start()

    for side in range(2):

        @pl.when(has[side])
        def _():
            for i in range(chips - 1):
                over(side, CHUNKS - 1, i).wait_recv()
                to_mate(side, CHUNKS - 1, i + 1).start()

    for side in range(2):

        @pl.when(has[side])
        def _():
            for j in range(CHUNKS):
                for i in range(chips):
                    to_mate(side, j, i).wait_recv()
                    to_mate(side, j, i).wait_send()
                for i in range(chips - 1):
                    over(side, j, i).wait_send()
                send(side, j).wait_send()
            cells_arrival(side).wait_recv()
            send_cells(side).wait_send()

    info_ref[width:, :] = dot32(jnp.ones((8, 128), jnp.float32), rhs_ref[...], NT)


def spread_kernel(chips, tiles, part_ref, out_ref, land, s1, r1, s2, r2, s3, r3, s4, r4):
    group, tile = lax.axis_index("tm"), lax.axis_index("tile")
    chip, core = group // 2, group % 2
    mate = group + 1 - 2 * core
    others = [((chip + i) % chips) * 2 + core for i in range(1, chips)]
    far = [(tile + d) % tiles for d in range(1, tiles)]

    barrier = pltpu.get_barrier_semaphore()
    for peer in others + [mate]:
        pl.semaphore_signal(barrier, inc=1, device_id={"tm": peer}, device_id_type=MESH)
    for peer in far:
        pl.semaphore_signal(barrier, inc=1, device_id={"tile": peer}, device_id_type=MESH)
    pl.semaphore_wait(barrier, chips + tiles - 1)

    def slot(g, t):
        return out_ref.at[g, t]

    def scatter(d):
        return remote(part_ref.at[far[d]], land.at[d], s1.at[d], r1.at[d], tile=far[d])

    def gather(d):
        return remote(slot(group, tile), slot(group, tile), s2.at[d], r2.at[d], tile=far[d])

    def held(d):
        return (tile - d + tiles) % tiles

    def over(d, i):
        place = slot(group, held(d))
        return remote(place, place, s3.at[d, i], r3.at[d, i], tm=others[i])

    def to_mate(d, i):
        place = slot(((chip - i + chips) % chips) * 2 + core, held(d))
        return remote(place, place, s4.at[d, i], r4.at[d, i], tm=mate)

    for d in range(tiles - 1):
        scatter(d).start()
    total = part_ref[tile]
    for d in range(tiles - 1):
        scatter(d).wait_recv()
        total = total + land[d]
    out_ref[group, tile] = total
    for d in range(tiles - 1):
        gather(d).start()
    for d in range(tiles):
        if d:
            gather(d - 1).wait_recv()
        for i in range(chips - 1):
            over(d, i).start()
        to_mate(d, 0).start()
    for d in range(tiles):
        for i in range(chips - 1):
            over(d, i).wait_recv()
            to_mate(d, i + 1).start()
    for d in range(tiles):
        for i in range(chips):
            to_mate(d, i).wait_recv()
            to_mate(d, i).wait_send()
        for i in range(chips - 1):
            over(d, i).wait_send()
    for d in range(tiles - 1):
        scatter(d).wait_send()
        gather(d).wait_send()


def stencil_kernel(
    tiles, block, basis_ref, d_ref, dx_ref, dy_ref, sea_ref, fringe_ref, halo_ref, info_ref, part_ref,
    prop_ref, turned, gf, gl, f1, l1, f2, l2, fh, fl, lh, ll
):
    width, rows, columns = basis_ref.shape
    halves = block // 8
    column = lax.broadcasted_iota(jnp.int32, (8, columns), 1)

    def cell(ref, i, r):
        if r < 0:
            line = fringe_ref[r + HALF, i : i + 1, :]
        elif r >= rows:
            line = fringe_ref[r - rows + HALF, i : i + 1, :]
        else:
            line = ref[r : r + 1, :]
        return jnp.broadcast_to(line.astype(jnp.float32), (8, columns))

    for r in range(-HALF, rows + HALF):
        d, dx, dy, sea = (
            cell(ref, i, r) for i, ref in enumerate((d_ref, dx_ref, dy_ref, sea_ref))
        )
        center = sea * (1.0 - 4.0 * d)
        east = sea * (d * (1.0 - dx))
        west = sea * (d * (1.0 + dx))
        north = jnp.where(column == columns - 1, 0.0, sea * (d * (1.0 - dy)))
        south = jnp.where(column == 0, 0.0, sea * (d * (1.0 + dy)))
        at = r + HALF - 1
        if 0 <= at < rows + 2 * (HALF - 1):
            for i, gain in enumerate((center, east, west, north, south)):
                gf[i, at] = gain
            gl[0, at] = center
            gl[3, at] = pltpu.roll(south, columns - 1, 1)
            gl[4, at] = pltpu.roll(north, 1, 1)
        if 0 <= at - 1 < rows + 2 * (HALF - 1):
            gl[1, at - 1] = west
        if 0 <= at + 1 < rows + 2 * (HALF - 1):
            gl[2, at + 1] = east

    def rolled(x):
        return pltpu.roll(x, columns - 1, 1), pltpu.roll(x, 1, 1)

    def update(g, r, center, east, west, north, south):
        return (
            g[0, r] * center + g[1, r] * east + g[2, r] * west + g[3, r] * north + g[4, r] * south
        )

    def fields(kb, _):
        k = pl.multiple_of(kb * block, block)

        def load(r, h):
            if r < 0:
                return halo_ref[r + HALF, pl.ds(k + 8 * h, 8), :]
            if r >= rows:
                return halo_ref[r - rows + HALF, pl.ds(k + 8 * h, 8), :]
            return turned[r, h]

        for h in range(halves):
            turned[:, h] = jnp.swapaxes(basis_ref[pl.ds(k + 8 * h, 8)], 0, 1)
        edge = HALF - 1
        before = [load(-edge - 1, h) for h in range(halves)]
        here = [load(-edge, h) for h in range(halves)]
        for r in range(-edge, rows + edge):
            after = [load(r + 1, h) for h in range(halves)]
            for h in range(halves):
                north, south = rolled(here[h])
                f1[r + edge, h] = update(gf, r + edge, here[h], after[h], before[h], north, south)
                l1[r + edge, h] = update(gl, r + edge, here[h], after[h], before[h], north, south)
            before, here = here, after
        for g, s1, s2, high, low in ((gf, f1, f2, fh, fl), (gl, l1, l2, lh, ll)):
            src, dst = s1, s2
            for step in range(1, HALF):
                reach = HALF - 1 - step
                before = [src[edge - reach - 1, h] for h in range(halves)]
                here = [src[edge - reach, h] for h in range(halves)]
                for r in range(-reach, rows + reach):
                    after = [src[r + 1 + edge, h] for h in range(halves)]
                    new = []
                    for h in range(halves):
                        north, south = rolled(here[h])
                        new.append(update(g, r + edge, here[h], after[h], before[h], north, south))
                    if step < HALF - 1:
                        for h in range(halves):
                            dst[r + edge, h] = new[h]
                    else:
                        a, b = split(jnp.concatenate(new, axis=0))
                        high[r, pl.ds(k, block), :] = a
                        low[r, pl.ds(k, block), :] = b
                    before, here = here, after
                src, dst = dst, src
        return 0

    lax.fori_loop(0, width // block, fields, 0)
    prop_ref[...] = jnp.zeros_like(prop_ref)

    def row(r, _):
        prop_ref[...] += (
            dot16(lh[r], fh[r], NT) + dot16(lh[r], fl[r], NT) + dot16(ll[r], fh[r], NT)
        )
        return 0

    lax.fori_loop(0, rows, row, 0)
    lines = width // tiles
    for n in range(tiles):
        part_ref[n, :lines, :] = prop_ref[n * lines : (n + 1) * lines, :]
        part_ref[n, lines : 2 * lines, :] = info_ref[n * lines : (n + 1) * lines, :]
        part_ref[n, 2 * lines :, :] = info_ref[width:, :]


def eye_of(n):
    i = lax.broadcasted_iota(jnp.int32, (n, n), 0)
    j = lax.broadcasted_iota(jnp.int32, (n, n), 1)
    return (i == j).astype(jnp.float32)


def invert(mats, invs, tmps):
    n = mats[0].shape[0]
    eye = eye_of(n)
    size = 0.0
    for a, x, t in zip(mats, invs, tmps):
        scale = 1.0 / jnp.max(jnp.sum(jnp.abs(a[...]), axis=0, keepdims=True))
        r = eye - scale * a[...]
        t[...] = r
        x[...] = scale * (eye + r)
        size = jnp.maximum(size, jnp.sum(r * r))

    def small(c):
        return jnp.logical_not(c[1] <= 1e-2) & (c[0] < 30)

    def grow(carry):
        it, _ = carry
        size = 0.0
        for x, t in zip(invs, tmps):
            r = t[...].astype(jnp.bfloat16)
            r = dot16(r, r, NN)
            t[...] = r
            x[...] += dot16(x[...].astype(jnp.bfloat16), r.astype(jnp.bfloat16), NN)
            size = jnp.maximum(size, jnp.sum(r * r))
        return it + 1, size

    lax.while_loop(small, grow, (0, size))

    def residual():
        size = 0.0
        for a, x, t in zip(mats, invs, tmps):
            r = eye - dot3(a[...], x[...])
            t[...] = r
            size = jnp.maximum(size, jnp.sum(r * r))
        return size

    def grow_exact(carry):
        it, _ = carry
        size = 0.0
        for x, t in zip(invs, tmps):
            r = dot32(t[...], t[...])
            t[...] = r
            x[...] += dot32(x[...], r)
            size = jnp.maximum(size, jnp.sum(r * r))
        return it + 1, size

    def again(_):
        size = 0.0
        for a, x, t in zip(mats, invs, tmps):
            scale = 1.0 / jnp.max(jnp.sum(jnp.abs(a[...]), axis=0, keepdims=True))
            r = eye - scale * a[...]
            t[...] = r
            x[...] = scale * (eye + r)
            size = jnp.maximum(size, jnp.sum(r * r))
        lax.while_loop(small, grow_exact, (0, size))
        return residual()

    size = residual()
    size = lax.cond(size <= 0.25, lambda v: v, again, size)

    def correct(carry):
        it, _ = carry
        for x, t in zip(invs, tmps):
            x[...] += dot3(x[...], t[...])
        return it + 1, residual()

    lax.while_loop(lambda c: (c[1] > 1e-6) & (c[0] < 6), correct, (0, size))
    for x, t in zip(invs, tmps):
        x[...] += dot3(x[...], t[...])


def join_kernel(
    groups, scale_prop, scale_obs, sums_ref, basis_ref, coeff_ref, field_ref, s, x, t, w, st, col
):
    n = sums_ref.shape[3]
    lines = n // sums_ref.shape[1]
    middle = groups // 2
    q = q_inverse
    eye = eye_of(n)

    def prop(g):
        return sums_ref[g, :, :lines, :].reshape(n, n) * scale_prop

    def diagonal(i):
        value = ridge * eye
        if i < groups:
            p = prop(i)
            value = value + q * dot3(p, p, TN)
        if i > 0:
            value = value + (q * eye + sums_ref[i - 1, :, lines : 2 * lines, :].reshape(n, n) * scale_obs)
            if i < groups:
                value = value + ridge * eye
        return value

    def right(i):
        if i == 0:
            return jnp.zeros((8, n), jnp.float32)
        return sums_ref[i - 1, 0, 2 * lines :, :] * scale_obs

    for i in range(groups + 1):
        s[i] = diagonal(i)
    vec = [right(i) for i in range(groups + 1)]
    for level in range(max(middle, groups - middle)):
        top = level if level < middle else None
        low = groups - level if groups - level > middle else None
        todo = [i for i in (top, low) if i is not None]
        invert([s.at[i] for i in todo], [x.at[i] for i in todo], [t.at[i] for i in todo])
        for i in todo:
            if i == top:
                p = prop(i)
                w[i] = q * dot3(x[i], p, NT)
                s[i + 1] -= q * dot3(p, w[i])
                vec[i + 1] = vec[i + 1] + dot32(vec[i], w[i])
            else:
                p = prop(i - 1)
                w[i] = q * dot3(x[i], p)
                s[i - 1] -= q * dot3(p, w[i], TN)
                vec[i - 1] = vec[i - 1] + dot32(vec[i], w[i])
    invert([s.at[middle]], [x.at[middle]], [t.at[middle]])
    state = {middle: dot32(vec[middle], x[middle])}
    for i in range(middle - 1, -1, -1):
        state[i] = dot32(vec[i], x[i]) + dot32(state[i + 1], w[i], NT)
    for i in range(middle + 1, groups + 1):
        state[i] = dot32(vec[i], x[i]) + dot32(state[i - 1], w[i], NT)
    for i in range(groups + 1):
        st[i] = state[i]
    group = lax.axis_index("tm")
    coeff_ref[0:1, :] = st[group][:1]
    end = st[group + 1]
    coeff_ref[1:2, :] = end[:1]
    col[...] = dot32(eye, end, NT)

    def add(j, total):
        k = pl.multiple_of(8 * j, 8)
        weights = col[pl.ds(k, 8), :]
        for i in range(8):
            total = total + weights[i : i + 1, 0:1] * basis_ref[k + i]
        return total

    field_ref[...] = lax.fori_loop(0, n // 8, add, jnp.zeros(field_ref.shape, jnp.float32))


VMEM = pltpu.VMEM


def shards(basis, diffusion, drift_x, drift_y, land_sea, obs_cells, obs_values):
    width, rows, columns = basis.shape
    nobs = obs_cells.shape[1]
    groups = lax.axis_size("tm")
    tiles = lax.axis_size("tile")
    chips = groups // 2
    cells = (diffusion[0], drift_x[0], drift_y[0], land_sea)
    share = width // groups
    DMA = pltpu.SemaphoreType.DMA
    whole = pl.BlockSpec(memory_space=VMEM)
    halo, fringe, info = pl.pallas_call(
        functools.partial(edge_kernel, chips, tiles),
        out_shape=(
            jax.ShapeDtypeStruct((2 * HALF, width, columns), jnp.float32),
            jax.ShapeDtypeStruct((2 * HALF, 8, columns), jnp.float32),
            jax.ShapeDtypeStruct((width + 8, width), jnp.float32),
        ),
        in_specs=[whole] * 7,
        out_specs=[whole] * 3,
        scratch_shapes=[VMEM((2 * HALF, share, columns), jnp.float32)]
        + [VMEM((2 * HALF, 8, columns), jnp.float32)]
        + [VMEM((2 * rows, columns), jnp.float32)]
        + [VMEM((width, 128), jnp.float32)]
        + [VMEM((rows, width, columns), jnp.bfloat16)] * 2
        + [DMA((2, CHUNKS))] * 2
        + [DMA((2,))] * 2
        + [DMA((2, CHUNKS, max(chips - 1, 1)))] * 2
        + [DMA((2, CHUNKS, chips))] * 2,
        compiler_params=pltpu.CompilerParams(
            vmem_limit_bytes=40 << 20, collective_id=0, has_side_effects=True
        ),
        name="edges",
    )(basis, *cells, obs_cells, obs_values)
    block = 16
    edge_rows = rows + 2 * (HALF - 1)
    lines = 2 * width // tiles + 8
    part = pl.pallas_call(
        functools.partial(stencil_kernel, tiles, block),
        out_shape=jax.ShapeDtypeStruct((tiles, lines, width), jnp.float32),
        in_specs=[whole] * 8,
        out_specs=pl.BlockSpec(memory_space=VMEM),
        scratch_shapes=[VMEM((width, width), jnp.float32)]
        + [VMEM((rows, block // 8, 8, columns), jnp.float32)]
        + [VMEM((5, edge_rows, 8, columns), jnp.float32)] * 2
        + [VMEM((edge_rows, block // 8, 8, columns), jnp.float32)] * 4
        + [VMEM((rows, width, columns), jnp.bfloat16)] * 4,
        compiler_params=pltpu.CompilerParams(vmem_limit_bytes=48 << 20),
        cost_estimate=pl.CostEstimate(
            flops=20000 * width * rows * columns,
            bytes_accessed=4 * width * rows * columns,
            transcendentals=0,
        ),
        name="propagate",
    )(basis, *cells, fringe, halo, info)

    sums = pl.pallas_call(
        functools.partial(spread_kernel, chips, tiles),
        out_shape=jax.ShapeDtypeStruct((groups, tiles, lines, width), jnp.float32),
        in_specs=[whole],
        out_specs=whole,
        scratch_shapes=[VMEM((tiles - 1, lines, width), jnp.float32)]
        + [DMA((tiles - 1,))] * 4
        + [DMA((tiles, max(chips - 1, 1)))] * 2
        + [DMA((tiles, chips))] * 2,
        compiler_params=pltpu.CompilerParams(
            vmem_limit_bytes=16 << 20, collective_id=1, has_side_effects=True
        ),
        name="spread",
    )(part)
    coeffs, end_fields = pl.pallas_call(
        functools.partial(
            join_kernel, groups, 1.0 / (rows * columns * tiles), 1.0 / nobs
        ),
        out_shape=(
            jax.ShapeDtypeStruct((2, width), jnp.float32),
            jax.ShapeDtypeStruct((rows, columns), jnp.float32),
        ),
        in_specs=[whole] * 2,
        out_specs=[whole] * 2,
        scratch_shapes=[VMEM((groups + 1, width, width), jnp.float32)] * 4
        + [VMEM((groups + 1, 8, width), jnp.float32), VMEM((width, 8), jnp.float32)],
        compiler_params=pltpu.CompilerParams(vmem_limit_bytes=40 << 20),
        name="join",
    )(sums, basis)
    return coeffs[None], end_fields[None]


def solution(mesh):
    in_specs = (
        P(None, "tile", None),
        P("tm", "tile", None),
        P("tm", "tile", None),
        P("tm", "tile", None),
        P("tile", None),
        P("tm", None),
        P("tm", None),
    )
    out_specs = (P("tm", None, None), P("tm", "tile", None))
    return jax.shard_map(shards, mesh=mesh, in_specs=in_specs, out_specs=out_specs, check_vma=False)
```
